32 devices in a mesh: row: 8 (over y, x, core), col: 4 (over z).
Axes of the slice: x: 2, y: 2, z: 4, core: 2. Of those that a mesh axis runs over, the one named last changes fastest.
Arguments:
- frames: float32 [64, 16384], P(None, ('row', 'col')), may hold values from -8 to 8
- start: float32 [32, 16384], P(None, ('row', 'col')), may hold values from -6 to 6
Outputs:
- basis: float32 [32, 16384], P(None, ('row', 'col'))
The draws below stay inside these ranges and needn't reach their ends.
All inputs are finite; a program needn't handle non-finite values.
Results may differ from the reference program's by a relative error of at most 0.0003.
Values sent between devices are 32-bit elements; how exact they have to be, the bound alone decides.
No kernel may reach another device: no remote copies, remote signals or barrier semaphores. Data moves between devices by JAX's collectives and lax.ppermute only.
A program may use at most 320 MiB of HBM per device.

```python
import math
import jax
import jax.numpy as jnp
from jax import lax

F = 64
KV = 32
FRAMES = 16384


def draw_frames(key, part):
    first_key, second_key, third_key, fourth_key = jax.random.split(key, 4)
    groups = 16
    labels = jax.random.randint(first_key, (FRAMES,), 0, groups)
    centers = jax.random.truncated_normal(second_key, -4.0, 4.0, (F, groups), jnp.float32)
    noise = jax.random.truncated_normal(third_key, -4.0, 4.0, (F, FRAMES), jnp.float32)
    spread = jnp.exp(jax.random.uniform(fourth_key, (FRAMES,), jnp.float32, math.log(0.3), math.log(1.0)))
    picked = jnp.take(centers, labels, axis=1)
    return picked + spread[None, :] * noise


def shard_levels(rng, extent, pieces, least, top_value):
    level, own = 1.0, jax.random.fold_in(rng, 6)
    for axis_at, blocks in pieces:
        steps = jnp.exp(jax.random.uniform(jax.random.fold_in(own, axis_at), (blocks,), jnp.float32, least / len(pieces), top_value / len(pieces)))
        level = level * jnp.repeat(steps, extent[axis_at] // blocks).reshape([-1 if axis == axis_at else 1 for axis in range(len(extent))])
    return level


def gaussian(stream_key, shape, width, most, cuts=(), kind=jnp.bfloat16):
    entries = width * jax.random.normal(stream_key, shape, jnp.float32)
    if cuts:
        entries = entries * shard_levels(stream_key, shape, cuts, -0.22, 0.18)
    return jnp.clip(entries, -most, most).astype(kind)


def setup_inputs(seed: int = 0) -> dict:
    arg_keys = jax.random.split(jax.random.key(seed), 3)
    return {
        "frames": draw_frames(jax.random.fold_in(arg_keys[2], 71), 0),
        "start": gaussian(arg_keys[1], (KV, FRAMES), 1.0, 6.0, ((1, 32),), jnp.float32),
    }


def build_block(block_points, block_squares, column_points, column_squares):
    products = lax.dot_general(block_points, column_points, (((0,), (0,)), ((), ())), precision=lax.Precision.HIGHEST)
    distance = block_squares[:, None] + column_squares[None, :] - 2.0 * products
    return jnp.exp(-distance / (0.5 * block_points.shape[0]))

def orthonormal(vectors):
    gram_matrix = jnp.dot(vectors, vectors.T, precision=lax.Precision.HIGHEST) / FRAMES
    factor = jnp.linalg.cholesky(gram_matrix)
    return jax.scipy.linalg.solve_triangular(factor, vectors, lower=True)

def reference(frames, start):
    block_size = math.gcd(FRAMES, 1024)
    block_count = FRAMES // block_size
    squares = jnp.sum(frames * frames, axis=0)
    indices = jnp.arange(block_count, dtype=jnp.int32)

    def kernel_part(index):
        first = (index * block_size).astype(jnp.int32)
        points = lax.dynamic_slice_in_dim(frames, first, block_size, 1)
        point_squares = lax.dynamic_slice_in_dim(squares, first, block_size, 0)
        return build_block(points, point_squares, frames, squares)

    def density_part(index):
        return jnp.sum(kernel_part(index), axis=1)
    density = lax.map(density_part, indices).reshape(FRAMES)
    inverse = 1.0 / density

    def degree_part(index):
        return jnp.dot(kernel_part(index), inverse, precision=lax.Precision.HIGHEST)
    degree = lax.map(degree_part, indices).reshape(FRAMES)

    def markov(vectors):
        scaled = vectors * inverse[None, :]

        def product_part(index):
            return lax.dot_general(scaled, kernel_part(index), (((1,), (1,)), ((), ())), precision=lax.Precision.HIGHEST)
        blocks = lax.map(product_part, indices)
        joined = jnp.transpose(blocks, (1, 0, 2)).reshape(vectors.shape[0], FRAMES)
        return joined / degree[None, :]
    grown_one = markov(start)
    basis_one = orthonormal(grown_one)
    grown_two = markov(basis_one)
    return orthonormal(grown_two)
```

```python
import functools
import math
import jax
import jax.numpy as jnp
from jax import lax
from jax.experimental import pallas as pl
from jax.experimental.pallas import tpu as pltpu
from jax.sharding import PartitionSpec as P

VMEM = pl.BlockSpec(memory_space=pltpu.VMEM)
ROWS_BY_COLUMNS = (((1,), (0,)), ((), ()))
ROWS_BY_ROWS = (((1,), (1,)), ((), ()))
RESIDENT_BYTES = 36 << 20
DEGREE_ROWS = 16


def call(body, out_shape, operands, scratch=(), limit=20 << 20, name=None):
    return pl.pallas_call(
        body,
        out_shape=out_shape,
        in_specs=[VMEM] * len(operands),
        out_specs=jax.tree.map(lambda _: VMEM, out_shape),
        scratch_shapes=list(scratch),
        compiler_params=pltpu.CompilerParams(vmem_limit_bytes=limit),
        name=name,
    )(*operands)


def f32(*shape):
    return jax.ShapeDtypeStruct(shape, jnp.float32)


def bf16(*shape):
    return jax.ShapeDtypeStruct(shape, jnp.bfloat16)


def halves(values):
    high = values.astype(jnp.bfloat16)
    return high, (values - high.astype(jnp.float32)).astype(jnp.bfloat16)


def thirds(values):
    high = values.astype(jnp.bfloat16).astype(jnp.float32)
    middle = (values - high).astype(jnp.bfloat16).astype(jnp.float32)
    return high, middle, values - high - middle


def build_kernel(*refs, row_parts, column_parts, tile_rows, tile_columns):
    row_refs = refs[:row_parts]
    column_refs = refs[row_parts : row_parts + column_parts]
    outs = refs[row_parts + column_parts :]
    high_refs, low_refs = outs[:row_parts], outs[row_parts : 2 * row_parts]
    sums_ref, left, right, totals = outs[2 * row_parts :]
    features, width = row_refs[0].shape
    columns = column_parts * width
    scale = math.sqrt(math.log2(math.e) / (0.25 * features))

    for part, ref in enumerate(row_refs):
        span = slice(part * width, (part + 1) * width)
        points = ref[...].T * scale
        high, low = halves(points)
        left[span, 0:features] = high
        left[span, features : 2 * features] = high
        left[span, 2 * features : 3 * features] = low
        first, second, third = thirds(0.5 * jnp.sum(points * points, axis=1, keepdims=True))
        lane = lax.broadcasted_iota(jnp.int32, (width, features), 1)
        tail = jnp.where(lane == 0, first, jnp.where(lane == 1, second, jnp.where(lane == 2, third, 0.0)))
        tail = jnp.where((lane > 2) & (lane < 6), -1.0, tail)
        left[span, 3 * features : 4 * features] = tail.astype(jnp.bfloat16)
    for part, ref in enumerate(column_refs):
        span = slice(part * width, (part + 1) * width)
        points = ref[...] * scale
        high, low = halves(points)
        right[0:features, span] = high
        right[features : 2 * features, span] = low
        right[2 * features : 3 * features, span] = high
        first, second, third = thirds(0.5 * jnp.sum(points * points, axis=0, keepdims=True))
        line = lax.broadcasted_iota(jnp.int32, (features, width), 0)
        tail = jnp.where(line == 3, first, jnp.where(line == 4, second, jnp.where(line == 5, third, 0.0)))
        tail = jnp.where(line < 3, -1.0, tail)
        right[3 * features : 4 * features, span] = tail.astype(jnp.bfloat16)

    for part in range(row_parts):
        high_ref, low_ref = high_refs[part], low_refs[part]

        def step(index, _):
            start = pl.multiple_of(index * tile_rows, tile_rows)
            points = left[pl.ds(part * width + start, tile_rows), :]
            total = jnp.zeros((tile_rows, 128), jnp.float32)
            for first in range(0, columns, tile_columns):
                exponent = lax.dot_general(
                    points,
                    right[:, first : first + tile_columns],
                    ROWS_BY_COLUMNS,
                    preferred_element_type=jnp.float32,
                )
                values = jnp.exp2(exponent)
                high = values.astype(jnp.bfloat16)
                high_ref[pl.ds(start, tile_rows), first : first + tile_columns] = high
                low_ref[pl.ds(start, tile_rows), first : first + tile_columns] = (
                    values - high.astype(jnp.float32)
                ).astype(jnp.bfloat16)
                for lane in range(0, tile_columns, 128):
                    total = total + values[:, lane : lane + 128]
            totals[pl.ds(start, tile_rows), :] = total
            return 0

        lax.fori_loop(0, width // tile_rows, step, 0)
        sums_ref[part : part + 1, :] = jnp.sum(totals[...].T, axis=0, keepdims=True)
    for part in range(row_parts, sums_ref.shape[0]):
        sums_ref[part : part + 1, :] = jnp.zeros((1, width), jnp.float32)


def build(row_pieces, column_pieces):
    features, width = row_pieces[0].shape
    row_parts, column_parts = len(row_pieces), len(column_pieces)
    columns = column_parts * width
    out_shape = (bf16(width, columns),) * (2 * row_parts) + (f32(-(-row_parts // 8) * 8, width),)
    outs = call(
        functools.partial(
            build_kernel, row_parts=row_parts, column_parts=column_parts, tile_rows=256, tile_columns=512
        ),
        out_shape,
        (*row_pieces, *column_pieces),
        scratch=(
            pltpu.VMEM((row_parts * width, 4 * features), jnp.bfloat16),
            pltpu.VMEM((4 * features, columns), jnp.bfloat16),
            pltpu.VMEM((width, 128), jnp.float32),
        ),
        name="build",
    )
    return outs[:row_parts], outs[row_parts : 2 * row_parts], outs[-1]


def sweep(weights, high_refs, low_refs, out_ref, tile):
    rows = weights.shape[0] // 2
    width = high_refs[0].shape[0]
    kept = out_ref.shape[0]
    for first in range(0, out_ref.shape[1], tile):
        span = slice(first, first + tile)
        total = None
        for part, (high_ref, low_ref) in enumerate(zip(high_refs, low_refs)):
            lines = slice(part * width, (part + 1) * width)
            both = lax.dot_general(
                weights[:, lines], high_ref[:, span], ROWS_BY_COLUMNS, preferred_element_type=jnp.float32
            )
            last = lax.dot_general(
                weights[0:rows, lines], low_ref[:, span], ROWS_BY_COLUMNS, preferred_element_type=jnp.float32
            )
            term = both[:kept] + both[rows : rows + kept] + last[:kept]
            total = term if total is None else total + term
        out_ref[:, span] = total


def first_kernel(*refs, parts, peers):
    sums_refs, start_refs = refs[:peers], refs[peers : peers + parts]
    high_refs = refs[peers + parts : peers + 2 * parts]
    low_refs = refs[peers + 2 * parts : peers + 3 * parts]
    out_ref, inverse_ref, weights = refs[peers + 3 * parts :]
    vectors, width = start_refs[0].shape
    rows = weights.shape[0] // 2
    for part in range(parts):
        span = slice(part * width, (part + 1) * width)
        density = sums_refs[0][part : part + 1, :]
        for peer in range(1, peers):
            density = density + sums_refs[peer][part ^ peer : (part ^ peer) + 1, :]
        inverse = 1.0 / density
        if part == 0:
            inverse_ref[...] = inverse
        line = lax.broadcasted_iota(jnp.int32, (rows - vectors, width), 0)
        for first, piece in (
            (0, start_refs[part][...] * inverse),
            (vectors, jnp.where(line == 0, inverse, 0.0)),
        ):
            high, low = halves(piece)
            last = first + piece.shape[0]
            weights[first:last, span] = high
            weights[rows + first : rows + last, span] = low
    sweep(weights, high_refs, low_refs, out_ref, 256)


def second_kernel(*refs, parts):
    piece_refs, high_refs, low_refs = refs[:parts], refs[parts : 2 * parts], refs[2 * parts : 3 * parts]
    out_ref, weights = refs[3 * parts :]
    vectors, width = piece_refs[0].shape
    for part in range(parts):
        span = slice(part * width, (part + 1) * width)
        high, low = halves(piece_refs[part][...])
        weights[0:vectors, span] = high
        weights[vectors:, span] = low
    sweep(weights, high_refs, low_refs, out_ref, 256)


def exact(left, right, dims):
    return lax.dot_general(
        left, right, dims, precision=lax.Precision.HIGHEST, preferred_element_type=jnp.float32
    )


def grown_kernel(*refs):
    inverse_ref, piece_refs, (grown_ref, gram_ref, degree_ref) = refs[0], refs[1:-3], refs[-3:]
    vectors = grown_ref.shape[0]
    total = piece_refs[0][...]
    for ref in piece_refs[1:]:
        total = total + ref[...]
    degree = total[vectors : vectors + 1, :]
    grown = total[0:vectors, :] / degree
    degree_ref[...] = degree
    grown_ref[...] = grown * inverse_ref[...]
    gram_ref[...] = exact(grown, grown, ROWS_BY_ROWS)


def inverse_factor(gram):
    size = gram.shape[0]
    line = lax.broadcasted_iota(jnp.int32, (size, size), 0)
    lane = lax.broadcasted_iota(jnp.int32, (size, size), 1)
    table = jnp.concatenate([gram, jnp.where(line == lane, 1.0, 0.0)], axis=1)
    wide_line = lax.broadcasted_iota(jnp.int32, (size, 2 * size), 0)
    pivots = jnp.zeros((size, 1), jnp.float32)
    tall_line = lax.broadcasted_iota(jnp.int32, (size, 1), 0)
    for step in range(size):
        row = table[step : step + 1, :]
        column = table[:, step : step + 1]
        pivot = row[:, step : step + 1]
        factor = jnp.where(tall_line > step, column * (1.0 / pivot), 0.0)
        pivots = jnp.where(tall_line == step, pivot, pivots)
        table = table - factor * row
    return table[:, size:] * lax.rsqrt(pivots)


def factor_kernel(*refs, count):
    gram = refs[0][...]
    for ref in refs[1:-1]:
        gram = gram + ref[...]
    refs[-1][...] = inverse_factor(gram * (1.0 / count))


def grown_two_kernel(*refs):
    factor_ref, degree_ref, piece_refs, (grown_ref, gram_ref) = refs[0], refs[1], refs[2:-2], refs[-2:]
    total = piece_refs[0][...]
    for ref in piece_refs[1:]:
        total = total + ref[...]
    grown = exact(factor_ref[...], total / degree_ref[...], ROWS_BY_COLUMNS)
    grown_ref[...] = grown
    gram_ref[...] = exact(grown, grown, ROWS_BY_ROWS)


def finish_kernel(*refs, count):
    grown_ref, gram_refs, out_ref = refs[0], refs[1:-1], refs[-1]
    gram = gram_refs[0][...]
    for ref in gram_refs[1:]:
        gram = gram + ref[...]
    out_ref[...] = exact(inverse_factor(gram * (1.0 / count)), grown_ref[...], ROWS_BY_COLUMNS)


def swap(values, axis, mask):
    size = lax.axis_size(axis)
    return lax.ppermute(values, axis, [(index, index ^ mask) for index in range(size)])


def resident_shards(frames, start):
    row_size, column_size = lax.axis_size("row"), lax.axis_size("col")
    count = frames.shape[1] * row_size * column_size
    vectors, width = start.shape
    far = range(2, row_size, 2)

    row_pieces = [frames] + [swap(frames, "col", q) for q in range(1, column_size)]
    column_pieces = {0: frames}
    for p in far:
        column_pieces[p] = swap(frames, "row", p)
    for p in range(0, row_size, 2):
        column_pieces[p ^ 1] = swap(column_pieces[p], "row", 1)
    starts = [start] + [swap(start, "col", q) for q in range(1, column_size)]

    highs, lows, sums = build(row_pieces, [column_pieces[p] for p in range(row_size)])
    all_sums = [sums] + [swap(sums, "col", q) for q in range(1, column_size)]

    def spread(product):
        pieces = [product[:, p * width : (p + 1) * width] for p in range(row_size)]
        others = swap(jnp.concatenate(pieces[1::2], axis=1), "row", 1)
        own = jnp.concatenate(pieces[0::2], axis=1) + others
        pieces = [own[:, p * width : (p + 1) * width] for p in range(row_size // 2)]
        return [pieces[0]] + [swap(pieces[p // 2], "row", p) for p in far]

    def total_gram(gram):
        gram = gram + swap(gram, "row", 1)
        gram = functools.reduce(jnp.add, [swap(gram, "row", p) for p in far], gram)
        return [gram] + [swap(gram, "col", q) for q in range(1, column_size)]

    rows = vectors + DEGREE_ROWS
    columns = row_size * width
    product, inverse = call(
        functools.partial(first_kernel, parts=column_size, peers=column_size),
        (f32(vectors + 8, columns), f32(1, width)),
        (*all_sums, *starts, *highs, *lows),
        scratch=(pltpu.VMEM((2 * rows, column_size * width), jnp.bfloat16),),
        name="first_product",
    )
    weighted, gram, degree = call(
        grown_kernel,
        (f32(vectors, width), f32(vectors, vectors), f32(1, width)),
        (inverse, *spread(product)),
        name="grown",
    )
    pieces = [weighted] + [swap(weighted, "col", q) for q in range(1, column_size)]
    grams = total_gram(gram)
    product = call(
        functools.partial(second_kernel, parts=column_size),
        f32(vectors, columns),
        (*pieces, *highs, *lows),
        scratch=(pltpu.VMEM((2 * vectors, column_size * width), jnp.bfloat16),),
        name="second_product",
    )
    factor = call(
        functools.partial(factor_kernel, count=count), f32(vectors, vectors), grams, name="first_factor"
    )
    grown_two, gram_two = call(
        grown_two_kernel,
        (f32(vectors, width), f32(vectors, vectors)),
        (factor, degree, *spread(product)),
        name="grown_two",
    )
    return call(
        functools.partial(finish_kernel, count=count),
        f32(vectors, width),
        (grown_two, *total_gram(gram_two)),
        name="finish",
    )


def build_block(block_points, block_squares, column_points, column_squares):
    products = lax.dot_general(
        block_points, column_points, (((0,), (0,)), ((), ())), precision=lax.Precision.HIGHEST
    )
    distance = block_squares[:, None] + column_squares[None, :] - 2.0 * products
    return jnp.exp(-distance / (0.5 * block_points.shape[0]))


def stored_shards(frames, start):
    block_points = lax.all_gather(frames, "col", axis=1, tiled=True)
    column_points = lax.all_gather(frames, "row", axis=1, tiled=True)
    block_squares = jnp.sum(block_points * block_points, axis=0)
    column_squares = jnp.sum(column_points * column_points, axis=0)
    frame_count = frames.shape[1] * lax.axis_size("row") * lax.axis_size("col")
    block_rows = block_points.shape[1]
    height = min(512, block_rows)
    stored = [
        build_block(
            block_points[:, first : first + height],
            block_squares[first : first + height],
            column_points,
            column_squares,
        )
        for first in range(0, block_rows, height)
    ]

    def settle(partial_value):
        return lax.psum_scatter(partial_value, "col", scatter_dimension=1, tiled=True)

    def kernel_product(weights):
        spread_weights = lax.all_gather(weights, "row", axis=1, tiled=True)
        return settle(
            jnp.concatenate([exact(spread_weights, part, ROWS_BY_ROWS) for part in stored], axis=1)
        )

    def orthonormal(vectors):
        gram = lax.psum(exact(vectors, vectors, ROWS_BY_ROWS), ("row", "col")) / frame_count
        return jax.scipy.linalg.solve_triangular(jnp.linalg.cholesky(gram), vectors, lower=True)

    sums = jnp.concatenate([jnp.sum(part, axis=1)[None, :] for part in stored], axis=1)
    inverse = 1.0 / settle(sums)
    degree = kernel_product(inverse)
    basis_one = orthonormal(kernel_product(start * inverse) / degree)
    return orthonormal(kernel_product(basis_one * inverse) / degree)


def shards(frames, start):
    row_size, column_size = lax.axis_size("row"), lax.axis_size("col")
    entries = row_size * column_size * frames.shape[1] ** 2
    powers = row_size & (row_size - 1) == 0 and column_size & (column_size - 1) == 0
    if powers and row_size > 1 and 4 * entries <= RESIDENT_BYTES:
        return resident_shards(frames, start)
    return stored_shards(frames, start)


def solution(mesh):
    return jax.shard_map(
        shards,
        mesh=mesh,
        in_specs=(P(None, ("row", "col")), P(None, ("row", "col"))),
        out_specs=P(None, ("row", "col")),
        check_vma=False,
    )
```

```python
import functools
import math
import jax
import jax.numpy as jnp
from jax import lax
from jax.experimental import pallas as pl
from jax.experimental.pallas import tpu as pltpu
from jax.sharding import PartitionSpec as P

VMEM = pl.BlockSpec(memory_space=pltpu.VMEM)
ROWS_BY_COLUMNS = (((1,), (0,)), ((), ()))
ROWS_BY_ROWS = (((1,), (1,)), ((), ()))
RESIDENT_BYTES = 36 << 20
DEGREE_ROWS = 16


def call(body, out_shape, operands, scratch=(), limit=20 << 20, flops=0, name=None):
    return pl.pallas_call(
        body,
        out_shape=out_shape,
        in_specs=[VMEM] * len(operands),
        out_specs=jax.tree.map(lambda _: VMEM, out_shape),
        scratch_shapes=list(scratch),
        compiler_params=pltpu.CompilerParams(vmem_limit_bytes=limit),
        cost_estimate=pl.CostEstimate(flops=flops, bytes_accessed=0, transcendentals=0) if flops else None,
        name=name,
    )(*operands)


def f32(*shape):
    return jax.ShapeDtypeStruct(shape, jnp.float32)


def bf16(*shape):
    return jax.ShapeDtypeStruct(shape, jnp.bfloat16)


def halves(values):
    high = values.astype(jnp.bfloat16)
    return high, (values - high.astype(jnp.float32)).astype(jnp.bfloat16)


def thirds(values):
    high = values.astype(jnp.bfloat16).astype(jnp.float32)
    middle = (values - high).astype(jnp.bfloat16).astype(jnp.float32)
    return high, middle, values - high - middle


def row_operand(points, left, span):
    width, features = points.shape
    high, low = halves(points)
    left[span, 0:features] = high
    left[span, features : 2 * features] = high
    left[span, 2 * features : 3 * features] = low
    first, second, third = thirds(0.5 * jnp.sum(points * points, axis=1, keepdims=True))
    lane = lax.broadcasted_iota(jnp.int32, (width, features), 1)
    tail = jnp.where(lane == 0, first, jnp.where(lane == 1, second, jnp.where(lane == 2, third, 0.0)))
    tail = jnp.where((lane > 2) & (lane < 6), -1.0, tail)
    left[span, 3 * features : 4 * features] = tail.astype(jnp.bfloat16)


def column_operand(points, right, span):
    features, width = points.shape
    high, low = halves(points)
    right[0:features, span] = high
    right[features : 2 * features, span] = low
    right[2 * features : 3 * features, span] = high
    first, second, third = thirds(0.5 * jnp.sum(points * points, axis=0, keepdims=True))
    line = lax.broadcasted_iota(jnp.int32, (features, width), 0)
    tail = jnp.where(line == 3, first, jnp.where(line == 4, second, jnp.where(line == 5, third, 0.0)))
    tail = jnp.where(line < 3, -1.0, tail)
    right[3 * features : 4 * features, span] = tail.astype(jnp.bfloat16)


def build_rows(left, right, high_refs, low_refs, totals, sums_ref, tile_rows=256, tile_columns=512):
    width, columns = high_refs[0].shape
    for part, (high_ref, low_ref) in enumerate(zip(high_refs, low_refs)):
        for start in range(0, width, tile_rows):
            lines = slice(start, start + tile_rows)
            points = left[part * width + start : part * width + start + tile_rows, :]
            total = jnp.zeros((tile_rows, 128), jnp.float32)
            for first in range(0, columns, tile_columns):
                span = slice(first, first + tile_columns)
                values = jnp.exp2(
                    lax.dot_general(
                        points, right[:, span], ROWS_BY_COLUMNS, preferred_element_type=jnp.float32
                    )
                )
                high = values.astype(jnp.bfloat16)
                high_ref[lines, span] = high
                low_ref[lines, span] = (values - high.astype(jnp.float32)).astype(jnp.bfloat16)
                for lane in range(0, tile_columns, 128):
                    total = total + values[:, lane : lane + 128]
            totals[lines, :] = total
        sums_ref[part : part + 1, :] = jnp.sum(totals[...].T, axis=0, keepdims=True)
    for part in range(len(high_refs), sums_ref.shape[0]):
        sums_ref[part : part + 1, :] = jnp.zeros((1, width), jnp.float32)


def point_scale(features):
    return math.sqrt(math.log2(math.e) / (0.25 * features))


def build_own_kernel(*refs, column_parts):
    column_refs, (high_ref, low_ref, sums_ref, right, left, totals) = refs[:column_parts], refs[column_parts:]
    features, width = column_refs[0].shape
    scale = point_scale(features)
    row_operand(column_refs[0][...].T * scale, left, slice(0, width))
    for part, ref in enumerate(column_refs):
        column_operand(ref[...] * scale, right, slice(part * width, (part + 1) * width))
    build_rows(left, right, [high_ref], [low_ref], totals, sums_ref)


def build_rest_kernel(*refs, parts):
    right, own_ref, row_refs = refs[0], refs[1], refs[2 : 2 + parts]
    high_refs, low_refs = refs[2 + parts : 2 + 2 * parts], refs[2 + 2 * parts : 2 + 3 * parts]
    sums_ref, left, totals = refs[2 + 3 * parts :]
    features, width = row_refs[0].shape
    scale = point_scale(features)
    for part, ref in enumerate(row_refs):
        row_operand(ref[...].T * scale, left, slice(part * width, (part + 1) * width))
    build_rows(left, right, high_refs, low_refs, totals, sums_ref)
    sums_ref[1 : 1 + parts, :] = sums_ref[0:parts, :]
    sums_ref[0:1, :] = own_ref[0:1, :]


def sweep(weights, high_refs, low_refs, out_ref, which, tile=256):
    rows = weights.shape[0] // 2
    width = high_refs[0].shape[0]
    kept = out_ref.shape[1]
    for place, block in enumerate(which):
        for first in range(0, width, tile):
            span = slice(block * width + first, block * width + first + tile)
            total = None
            for part, (high_ref, low_ref) in enumerate(zip(high_refs, low_refs)):
                lines = slice(part * width, (part + 1) * width)
                both = lax.dot_general(
                    weights[:, lines], high_ref[:, span], ROWS_BY_COLUMNS, preferred_element_type=jnp.float32
                )
                last = lax.dot_general(
                    weights[0:rows, lines], low_ref[:, span], ROWS_BY_COLUMNS, preferred_element_type=jnp.float32
                )
                term = both[:kept] + both[rows : rows + kept] + last[:kept]
                total = term if total is None else total + term
            out_ref[place, :, first : first + tile] = total


def first_kernel(*refs, parts, peers, which):
    sums_refs, start_refs = refs[:peers], refs[peers : peers + parts]
    high_refs = refs[peers + parts : peers + 2 * parts]
    low_refs = refs[peers + 2 * parts : peers + 3 * parts]
    out_ref, inverse_ref, weights = refs[peers + 3 * parts :]
    vectors, width = start_refs[0].shape
    rows = weights.shape[0] // 2
    for part in range(parts):
        span = slice(part * width, (part + 1) * width)
        density = sums_refs[0][part : part + 1, :]
        for peer in range(1, peers):
            density = density + sums_refs[peer][part ^ peer : (part ^ peer) + 1, :]
        inverse = 1.0 / density
        if part == 0:
            inverse_ref[...] = inverse
        line = lax.broadcasted_iota(jnp.int32, (rows - vectors, width), 0)
        for first, piece in (
            (0, start_refs[part][...] * inverse),
            (vectors, jnp.where(line == 0, inverse, 0.0)),
        ):
            high, low = halves(piece)
            last = first + piece.shape[0]
            weights[first:last, span] = high
            weights[rows + first : rows + last, span] = low
    sweep(weights, high_refs, low_refs, out_ref, which)


def again_kernel(*refs, parts, which):
    weights, high_refs, low_refs, out_ref = refs[0], refs[1 : 1 + parts], refs[1 + parts : -1], refs[-1]
    sweep(weights, high_refs, low_refs, out_ref, which)


def second_kernel(*refs, parts, which):
    piece_refs, high_refs, low_refs = refs[:parts], refs[parts : 2 * parts], refs[2 * parts : 3 * parts]
    out_ref, gram_ref, weights = refs[3 * parts :]
    vectors, width = piece_refs[0].shape[0], high_refs[0].shape[0]
    gram = piece_refs[0][:, width:]
    for ref in piece_refs[1:]:
        gram = gram + ref[:, width:]
    gram_ref[...] = gram
    for part in range(parts):
        span = slice(part * width, (part + 1) * width)
        high, low = halves(piece_refs[part][:, 0:width])
        weights[0:vectors, span] = high
        weights[vectors:, span] = low
    sweep(weights, high_refs, low_refs, out_ref, which)
    for place in range(len(which)):
        out_ref[place, :, width:] = gram


def second_again_kernel(*refs, parts, which):
    weights, gram_ref = refs[0], refs[1]
    high_refs, low_refs, out_ref = refs[2 : 2 + parts], refs[2 + parts : -1], refs[-1]
    sweep(weights, high_refs, low_refs, out_ref, which)
    width = high_refs[0].shape[0]
    for place in range(len(which)):
        out_ref[place, :, width:] = gram_ref[...]


def exact(left, right, dims):
    return lax.dot_general(
        left, right, dims, precision=lax.Precision.HIGHEST, preferred_element_type=jnp.float32
    )


def grown_kernel(*refs):
    inverse_ref, piece_refs, (grown_ref, degree_ref) = refs[0], refs[1:-2], refs[-2:]
    vectors = grown_ref.shape[0]
    width = degree_ref.shape[1]
    total = piece_refs[0][...]
    for ref in piece_refs[1:]:
        total = total + ref[...]
    degree = total[vectors : vectors + 1, :]
    grown = total[0:vectors, :] / degree
    degree_ref[...] = degree
    grown_ref[:, 0:width] = grown * inverse_ref[...]
    gram = exact(grown, grown, ROWS_BY_ROWS)
    grown_ref[:, width:] = jnp.concatenate([gram, jnp.zeros((vectors, 128 - vectors), jnp.float32)], axis=1)


def inverse_factor(gram, panel=16):
    size = gram.shape[0]
    shape = (size, 2 * size)
    line = lax.broadcasted_iota(jnp.int32, (size, size), 0)
    lane = lax.broadcasted_iota(jnp.int32, (size, size), 1)
    table = jnp.concatenate([gram, jnp.where(line == lane, 1.0, 0.0)], axis=1)
    tall = lax.broadcasted_iota(jnp.int32, shape, 0)
    pivots = jnp.zeros(shape, jnp.float32)
    for first in range(0, size, panel):
        columns = [jnp.broadcast_to(table[:, step : step + 1], shape) for step in range(first, first + panel)]
        for place, step in enumerate(range(first, first + panel)):
            pivot = columns[place][step : step + 1, :]
            pivots = jnp.where(tall == step, pivot, pivots)
            factor = jnp.where(tall > step, columns[place] * (1.0 / pivot), 0.0)
            for later in range(place + 1, panel):
                columns[later] = columns[later] - factor * columns[later][step : step + 1, :]
            table = table - factor * table[step : step + 1, :]
    return table[:, size:] * lax.rsqrt(pivots[:, size:])


def grown_two_kernel(*refs, count):
    degree_ref, piece_refs, (grown_ref, gram_ref) = refs[0], refs[1:-2], refs[-2:]
    vectors, width = grown_ref.shape
    total = piece_refs[0][...]
    for ref in piece_refs[1:]:
        total = total + ref[...]
    factor = inverse_factor(total[:, width : width + vectors] * (1.0 / count))
    grown = exact(factor, total[:, 0:width] / degree_ref[...], ROWS_BY_COLUMNS)
    grown_ref[...] = grown
    gram_ref[...] = exact(grown, grown, ROWS_BY_ROWS)


def finish_kernel(*refs, count):
    grown_ref, gram_refs, out_ref = refs[0], refs[1:-1], refs[-1]
    gram = gram_refs[0][...]
    for ref in gram_refs[1:]:
        gram = gram + ref[...]
    out_ref[...] = exact(inverse_factor(gram * (1.0 / count)), grown_ref[...], ROWS_BY_COLUMNS)


def swap(values, axis, mask):
    size = lax.axis_size(axis)
    return lax.ppermute(values, axis, [(index, index ^ mask) for index in range(size)])


def resident_shards(frames, start):
    row_size, column_size = lax.axis_size("row"), lax.axis_size("col")
    count = frames.shape[1] * row_size * column_size
    features, width = frames.shape
    vectors = start.shape[0]
    columns = row_size * width
    near, far = range(1, column_size), range(2, row_size, 2)
    even, odd = range(0, row_size, 2), range(1, row_size, 2)

    row_pieces = [swap(frames, "col", q) for q in near]
    even_pieces = [frames] + [swap(frames, "row", p) for p in far]
    odd_pieces = swap(jnp.stack(even_pieces), "row", 1)
    column_pieces = [(odd_pieces[p // 2] if p % 2 else even_pieces[p // 2]) for p in range(row_size)]
    starts = [start] + [swap(start, "col", q) for q in near]

    operands = 4 * features
    work = 2 * width * columns * operands
    totals = pltpu.VMEM((width, 128), jnp.float32)
    high, low, own_sums, right = call(
        functools.partial(build_own_kernel, column_parts=row_size),
        (bf16(width, columns), bf16(width, columns), f32(8, width), bf16(operands, columns)),
        column_pieces,
        scratch=(pltpu.VMEM((width, operands), jnp.bfloat16), totals),
        flops=2 * work,
        name="build_own",
    )
    rest = len(row_pieces)
    *blocks, sums = call(
        functools.partial(build_rest_kernel, parts=rest),
        (bf16(width, columns),) * (2 * rest) + (f32(8, width),),
        (right, own_sums, *row_pieces),
        scratch=(pltpu.VMEM((rest * width, operands), jnp.bfloat16), totals),
        flops=2 * rest * work,
        name="build_rest",
    )
    stored = (high, *blocks[:rest], low, *blocks[rest:])
    all_sums = [sums] + [swap(sums, "col", q) for q in near]

    def spread(evens, odds):
        own = evens + swap(odds, "row", 1)
        return [own[0]] + [swap(own[p // 2], "row", p) for p in far]

    def total_gram(gram):
        gram = gram + swap(gram, "row", 1)
        gram = functools.reduce(jnp.add, [swap(gram, "row", p) for p in far], gram)
        return [gram] + [swap(gram, "col", q) for q in near]

    rows = vectors + DEGREE_ROWS
    work = 2 * 3 * rows * column_size * width * columns
    odds, inverse, weights = call(
        functools.partial(first_kernel, parts=column_size, peers=column_size, which=odd),
        (f32(len(odd), vectors + 8, width), f32(1, width), bf16(2 * rows, column_size * width)),
        (*all_sums, *starts, *stored),
        flops=work,
        name="first_odd",
    )
    evens = call(
        functools.partial(again_kernel, parts=column_size, which=even),
        f32(len(even), vectors + 8, width),
        (weights, *stored),
        flops=work,
        name="first_even",
    )
    weighted, degree = call(
        grown_kernel, (f32(vectors, width + 128), f32(1, width)), (inverse, *spread(evens, odds)), name="grown"
    )
    pieces = [weighted] + [swap(weighted, "col", q) for q in near]
    odds, gram, weights = call(
        functools.partial(second_kernel, parts=column_size, which=odd),
        (f32(len(odd), vectors, width + 128), f32(vectors, 128), bf16(2 * vectors, column_size * width)),
        (*pieces, *stored),
        flops=work,
        name="second_odd",
    )
    evens = call(
        functools.partial(second_again_kernel, parts=column_size, which=even),
        f32(len(even), vectors, width + 128),
        (weights, gram, *stored),
        flops=work,
        name="second_even",
    )
    grown_two, gram_two = call(
        functools.partial(grown_two_kernel, count=count),
        (f32(vectors, width), f32(vectors, vectors)),
        (degree, *spread(evens, odds)),
        name="grown_two",
    )
    return call(
        functools.partial(finish_kernel, count=count),
        f32(vectors, width),
        (grown_two, *total_gram(gram_two)),
        name="finish",
    )


def build_block(block_points, block_squares, column_points, column_squares):
    products = lax.dot_general(
        block_points, column_points, (((0,), (0,)), ((), ())), precision=lax.Precision.HIGHEST
    )
    distance = block_squares[:, None] + column_squares[None, :] - 2.0 * products
    return jnp.exp(-distance / (0.5 * block_points.shape[0]))


def stored_shards(frames, start):
    block_points = lax.all_gather(frames, "col", axis=1, tiled=True)
    column_points = lax.all_gather(frames, "row", axis=1, tiled=True)
    block_squares = jnp.sum(block_points * block_points, axis=0)
    column_squares = jnp.sum(column_points * column_points, axis=0)
    frame_count = frames.shape[1] * lax.axis_size("row") * lax.axis_size("col")
    block_rows = block_points.shape[1]
    height = min(512, block_rows)
    stored = [
        build_block(
            block_points[:, first : first + height],
            block_squares[first : first + height],
            column_points,
            column_squares,
        )
        for first in range(0, block_rows, height)
    ]

    def settle(partial_value):
        return lax.psum_scatter(partial_value, "col", scatter_dimension=1, tiled=True)

    def kernel_product(weights):
        spread_weights = lax.all_gather(weights, "row", axis=1, tiled=True)
        return settle(
            jnp.concatenate([exact(spread_weights, part, ROWS_BY_ROWS) for part in stored], axis=1)
        )

    def orthonormal(vectors):
        gram = lax.psum(exact(vectors, vectors, ROWS_BY_ROWS), ("row", "col")) / frame_count
        return jax.scipy.linalg.solve_triangular(jnp.linalg.cholesky(gram), vectors, lower=True)

    sums = jnp.concatenate([jnp.sum(part, axis=1)[None, :] for part in stored], axis=1)
    inverse = 1.0 / settle(sums)
    degree = kernel_product(inverse)
    basis_one = orthonormal(kernel_product(start * inverse) / degree)
    return orthonormal(kernel_product(basis_one * inverse) / degree)


def shards(frames, start):
    row_size, column_size = lax.axis_size("row"), lax.axis_size("col")
    entries = row_size * column_size * frames.shape[1] ** 2
    powers = row_size & (row_size - 1) == 0 and column_size & (column_size - 1) == 0
    if powers and row_size > 1 and 4 * entries <= RESIDENT_BYTES:
        return resident_shards(frames, start)
    return stored_shards(frames, start)


def solution(mesh):
    return jax.shard_map(
        shards,
        mesh=mesh,
        in_specs=(P(None, ("row", "col")), P(None, ("row", "col"))),
        out_specs=P(None, ("row", "col")),
        check_vma=False,
    )
```

```python
import functools
import math
import jax
import jax.numpy as jnp
from jax import lax
from jax.experimental import pallas as pl
from jax.experimental.pallas import tpu as pltpu
from jax.sharding import PartitionSpec as P

VMEM = pl.BlockSpec(memory_space=pltpu.VMEM)
ROWS_BY_COLUMNS = (((1,), (0,)), ((), ()))
ROWS_BY_ROWS = (((1,), (1,)), ((), ()))
RESIDENT_BYTES = 36 << 20
DEGREE_ROWS = 16


def call(body, out_shape, operands, scratch=(), limit=20 << 20, flops=0, name=None):
    return pl.pallas_call(
        body,
        out_shape=out_shape,
        in_specs=[VMEM] * len(operands),
        out_specs=jax.tree.map(lambda _: VMEM, out_shape),
        scratch_shapes=list(scratch),
        compiler_params=pltpu.CompilerParams(vmem_limit_bytes=limit),
        cost_estimate=pl.CostEstimate(flops=flops, bytes_accessed=0, transcendentals=0) if flops else None,
        name=name,
    )(*operands)


def f32(*shape):
    return jax.ShapeDtypeStruct(shape, jnp.float32)


def bf16(*shape):
    return jax.ShapeDtypeStruct(shape, jnp.bfloat16)


def halves(values):
    high = values.astype(jnp.bfloat16)
    return high, (values - high.astype(jnp.float32)).astype(jnp.bfloat16)


def thirds(values):
    high = values.astype(jnp.bfloat16).astype(jnp.float32)
    middle = (values - high).astype(jnp.bfloat16).astype(jnp.float32)
    return high, middle, values - high - middle


def row_operand(points, left, span):
    width, features = points.shape
    high, low = halves(points)
    left[span, 0:features] = high
    left[span, features : 2 * features] = high
    left[span, 2 * features : 3 * features] = low
    first, second, third = thirds(0.5 * jnp.sum(points * points, axis=1, keepdims=True))
    lane = lax.broadcasted_iota(jnp.int32, (width, features), 1)
    tail = jnp.where(lane == 0, first, jnp.where(lane == 1, second, jnp.where(lane == 2, third, 0.0)))
    tail = jnp.where((lane > 2) & (lane < 6), -1.0, tail)
    left[span, 3 * features : 4 * features] = tail.astype(jnp.bfloat16)


def column_operand(points, right, span):
    features, width = points.shape
    high, low = halves(points)
    right[0:features, span] = high
    right[features : 2 * features, span] = low
    right[2 * features : 3 * features, span] = high
    first, second, third = thirds(0.5 * jnp.sum(points * points, axis=0, keepdims=True))
    line = lax.broadcasted_iota(jnp.int32, (features, width), 0)
    tail = jnp.where(line == 3, first, jnp.where(line == 4, second, jnp.where(line == 5, third, 0.0)))
    tail = jnp.where(line < 3, -1.0, tail)
    right[3 * features : 4 * features, span] = tail.astype(jnp.bfloat16)


def build_rows(left, right, high_refs, low_refs, totals, sums_ref, tile_rows=256, tile_columns=512):
    width, columns = high_refs[0].shape
    for part, (high_ref, low_ref) in enumerate(zip(high_refs, low_refs)):
        for start in range(0, width, tile_rows):
            lines = slice(start, start + tile_rows)
            points = left[part * width + start : part * width + start + tile_rows, :]
            total = jnp.zeros((tile_rows, 128), jnp.float32)
            for first in range(0, columns, tile_columns):
                span = slice(first, first + tile_columns)
                values = jnp.exp2(
                    lax.dot_general(
                        points, right[:, span], ROWS_BY_COLUMNS, preferred_element_type=jnp.float32
                    )
                )
                high = values.astype(jnp.bfloat16)
                high_ref[lines, span] = high
                low_ref[lines, span] = (values - high.astype(jnp.float32)).astype(jnp.bfloat16)
                for lane in range(0, tile_columns, 128):
                    total = total + values[:, lane : lane + 128]
            totals[lines, :] = total
        sums_ref[part : part + 1, :] = jnp.sum(totals[...].T, axis=0, keepdims=True)
    for part in range(len(high_refs), sums_ref.shape[0]):
        sums_ref[part : part + 1, :] = jnp.zeros((1, width), jnp.float32)


def point_scale(features):
    return math.sqrt(math.log2(math.e) / (0.25 * features))


def build_even_kernel(*refs, row_parts, column_parts):
    row_refs, column_refs = refs[:row_parts], (refs[0], *refs[row_parts : row_parts + column_parts - 1])
    outs = refs[row_parts + column_parts - 1 :]
    high_refs, low_refs = outs[:row_parts], outs[row_parts : 2 * row_parts]
    sums_ref, left, right, totals = outs[2 * row_parts :]
    features, width = row_refs[0].shape
    scale = point_scale(features)
    for part, ref in enumerate(row_refs):
        row_operand(ref[...].T * scale, left, slice(part * width, (part + 1) * width))
    for part, ref in enumerate(column_refs):
        column_operand(ref[...] * scale, right, slice(part * width, (part + 1) * width))
    build_rows(left, right, high_refs, low_refs, totals, sums_ref)


def build_odd_kernel(*refs, row_parts, column_parts):
    left, even_ref, start_ref, column_refs = refs[0], refs[1], refs[2], refs[3 : 3 + column_parts]
    outs = refs[3 + column_parts :]
    high_refs, low_refs = outs[:row_parts], outs[row_parts : 2 * row_parts]
    packed_ref, right, totals, sums_ref = outs[2 * row_parts :]
    features, width = column_refs[0].shape
    vectors = start_ref.shape[0]
    scale = point_scale(features)
    for part, ref in enumerate(column_refs):
        column_operand(ref[...] * scale, right, slice(part * width, (part + 1) * width))
    build_rows(left, right, high_refs, low_refs, totals, sums_ref)
    packed_ref[0:vectors, :] = start_ref[...]
    packed_ref[vectors:, :] = sums_ref[...] + even_ref[...]


def sweep(weights, high_refs, low_refs, out_ref, tile=256):
    rows = weights.shape[0] // 2
    width = high_refs[0].shape[0]
    kept = out_ref.shape[1]
    for block in range(out_ref.shape[0]):
        for first in range(0, width, tile):
            span = slice(block * width + first, block * width + first + tile)
            total = None
            for part, (high_ref, low_ref) in enumerate(zip(high_refs, low_refs)):
                lines = slice(part * width, (part + 1) * width)
                both = lax.dot_general(
                    weights[:, lines], high_ref[:, span], ROWS_BY_COLUMNS, preferred_element_type=jnp.float32
                )
                last = lax.dot_general(
                    weights[0:rows, lines], low_ref[:, span], ROWS_BY_COLUMNS, preferred_element_type=jnp.float32
                )
                term = both[:kept] + both[rows : rows + kept] + last[:kept]
                total = term if total is None else total + term
            out_ref[block, :, first : first + tile] = total


def first_kernel(*refs, parts):
    packed_refs, high_refs, low_refs = refs[:parts], refs[parts : 2 * parts], refs[2 * parts : 3 * parts]
    out_ref, inverse_ref, weights = refs[3 * parts :]
    rows = weights.shape[0] // 2
    vectors = rows - DEGREE_ROWS
    width = packed_refs[0].shape[1]
    for part in range(parts):
        span = slice(part * width, (part + 1) * width)
        density = packed_refs[0][vectors + part : vectors + part + 1, :]
        for peer in range(1, parts):
            line = vectors + (part ^ peer)
            density = density + packed_refs[peer][line : line + 1, :]
        inverse = 1.0 / density
        if part == 0:
            inverse_ref[...] = inverse
        line = lax.broadcasted_iota(jnp.int32, (DEGREE_ROWS, width), 0)
        for first, piece in (
            (0, packed_refs[part][0:vectors, :] * inverse),
            (vectors, jnp.where(line == 0, inverse, 0.0)),
        ):
            high, low = halves(piece)
            last = first + piece.shape[0]
            weights[first:last, span] = high
            weights[rows + first : rows + last, span] = low
    sweep(weights, high_refs, low_refs, out_ref)


def again_kernel(*refs, parts):
    weights, high_refs, low_refs, out_ref = refs[0], refs[1 : 1 + parts], refs[1 + parts : -1], refs[-1]
    sweep(weights, high_refs, low_refs, out_ref)


def second_kernel(*refs, parts):
    piece_refs, high_refs, low_refs = refs[:parts], refs[parts : 2 * parts], refs[2 * parts : 3 * parts]
    out_ref, gram_ref, weights = refs[3 * parts :]
    vectors, width = piece_refs[0].shape[0], high_refs[0].shape[0]
    gram = piece_refs[0][:, width:]
    for ref in piece_refs[1:]:
        gram = gram + ref[:, width:]
    gram_ref[...] = gram
    for part in range(parts):
        span = slice(part * width, (part + 1) * width)
        high, low = halves(piece_refs[part][:, 0:width])
        weights[0:vectors, span] = high
        weights[vectors:, span] = low
    sweep(weights, high_refs, low_refs, out_ref)
    for block in range(out_ref.shape[0]):
        out_ref[block, :, width:] = gram


def second_again_kernel(*refs, parts):
    weights, gram_ref = refs[0], refs[1]
    high_refs, low_refs, out_ref = refs[2 : 2 + parts], refs[2 + parts : -1], refs[-1]
    sweep(weights, high_refs, low_refs, out_ref)
    width = high_refs[0].shape[0]
    for block in range(out_ref.shape[0]):
        out_ref[block, :, width:] = gram_ref[...]


def exact(left, right, dims):
    return lax.dot_general(
        left, right, dims, precision=lax.Precision.HIGHEST, preferred_element_type=jnp.float32
    )


def grown_kernel(*refs):
    inverse_ref, piece_refs, (grown_ref, degree_ref) = refs[0], refs[1:-2], refs[-2:]
    vectors = grown_ref.shape[0]
    width = degree_ref.shape[1]
    total = piece_refs[0][...]
    for ref in piece_refs[1:]:
        total = total + ref[...]
    degree = total[vectors : vectors + 1, :]
    grown = total[0:vectors, :] / degree
    degree_ref[...] = degree
    grown_ref[:, 0:width] = grown * inverse_ref[...]
    gram = exact(grown, grown, ROWS_BY_ROWS)
    grown_ref[:, width:] = jnp.concatenate([gram, jnp.zeros((vectors, 128 - vectors), jnp.float32)], axis=1)


def inverse_factor(gram, panel=16):
    size = gram.shape[0]
    shape = (size, 2 * size)
    line = lax.broadcasted_iota(jnp.int32, (size, size), 0)
    lane = lax.broadcasted_iota(jnp.int32, (size, size), 1)
    table = jnp.concatenate([gram, jnp.where(line == lane, 1.0, 0.0)], axis=1)
    tall = lax.broadcasted_iota(jnp.int32, shape, 0)
    pivots = jnp.zeros(shape, jnp.float32)
    for first in range(0, size, panel):
        columns = [jnp.broadcast_to(table[:, step : step + 1], shape) for step in range(first, first + panel)]
        for place, step in enumerate(range(first, first + panel)):
            pivot = columns[place][step : step + 1, :]
            pivots = jnp.where(tall == step, pivot, pivots)
            factor = jnp.where(tall > step, columns[place] * (1.0 / pivot), 0.0)
            for later in range(place + 1, panel):
                columns[later] = columns[later] - factor * columns[later][step : step + 1, :]
            table = table - factor * table[step : step + 1, :]
    return table[:, size:] * lax.rsqrt(pivots[:, size:])


def grown_two_kernel(*refs, count):
    degree_ref, piece_refs, (grown_ref, gram_ref) = refs[0], refs[1:-2], refs[-2:]
    vectors, width = grown_ref.shape
    total = piece_refs[0][...]
    for ref in piece_refs[1:]:
        total = total + ref[...]
    factor = inverse_factor(total[:, width : width + vectors] * (1.0 / count))
    grown = exact(factor, total[:, 0:width] / degree_ref[...], ROWS_BY_COLUMNS)
    grown_ref[...] = grown
    gram_ref[...] = exact(grown, grown, ROWS_BY_ROWS)


def finish_kernel(*refs, count):
    grown_ref, gram_refs, out_ref = refs[0], refs[1:-1], refs[-1]
    gram = gram_refs[0][...]
    for ref in gram_refs[1:]:
        gram = gram + ref[...]
    out_ref[...] = exact(inverse_factor(gram * (1.0 / count)), grown_ref[...], ROWS_BY_COLUMNS)


def swap(values, axis, mask):
    size = lax.axis_size(axis)
    return lax.ppermute(values, axis, [(index, index ^ mask) for index in range(size)])


def resident_shards(frames, start):
    row_size, column_size = lax.axis_size("row"), lax.axis_size("col")
    count = frames.shape[1] * row_size * column_size
    features, width = frames.shape
    vectors = start.shape[0]
    half = row_size // 2
    columns = half * width
    near, far = range(1, column_size), range(2, row_size, 2)

    row_pieces = [frames] + [swap(frames, "col", q) for q in near]
    even_pieces = [swap(frames, "row", p) for p in far]
    odd_pieces = [swap(piece, "row", 1) for piece in (frames, *even_pieces)]

    operands = 4 * features
    height = column_size * width
    work = 2 * 2 * height * columns * operands
    stored = (bf16(width, columns),) * (2 * column_size)
    totals = pltpu.VMEM((width, 128), jnp.float32)
    *even, sums, left = call(
        functools.partial(build_even_kernel, row_parts=column_size, column_parts=half),
        (*stored, f32(8, width), bf16(height, operands)),
        (*row_pieces, *even_pieces),
        scratch=(pltpu.VMEM((operands, columns), jnp.bfloat16), totals),
        flops=work,
        name="build_even",
    )
    *odd, packed = call(
        functools.partial(build_odd_kernel, row_parts=column_size, column_parts=half),
        (*stored, f32(vectors + 8, width)),
        (left, sums, start, *odd_pieces),
        scratch=(
            pltpu.VMEM((operands, columns), jnp.bfloat16),
            totals,
            pltpu.VMEM((8, width), jnp.float32),
        ),
        flops=work,
        name="build_odd",
    )
    all_packed = [packed] + [swap(packed, "col", q) for q in near]

    def spread(evens, odds):
        own = evens + swap(odds, "row", 1)
        return [own[0]] + [swap(own[p // 2], "row", p) for p in far]

    def total_gram(gram):
        gram = gram + swap(gram, "row", 1)
        gram = functools.reduce(jnp.add, [swap(gram, "row", p) for p in far], gram)
        return [gram] + [swap(gram, "col", q) for q in near]

    rows = vectors + DEGREE_ROWS
    work = 2 * 3 * rows * height * columns
    odds, inverse, weights = call(
        functools.partial(first_kernel, parts=column_size),
        (f32(half, vectors + 8, width), f32(1, width), bf16(2 * rows, height)),
        (*all_packed, *odd),
        flops=work,
        name="first_odd",
    )
    evens = call(
        functools.partial(again_kernel, parts=column_size),
        f32(half, vectors + 8, width),
        (weights, *even),
        flops=work,
        name="first_even",
    )
    weighted, degree = call(
        grown_kernel, (f32(vectors, width + 128), f32(1, width)), (inverse, *spread(evens, odds)), name="grown"
    )
    pieces = [weighted] + [swap(weighted, "col", q) for q in near]
    odds, gram, weights = call(
        functools.partial(second_kernel, parts=column_size),
        (f32(half, vectors, width + 128), f32(vectors, 128), bf16(2 * vectors, height)),
        (*pieces, *odd),
        flops=work,
        name="second_odd",
    )
    evens = call(
        functools.partial(second_again_kernel, parts=column_size),
        f32(half, vectors, width + 128),
        (weights, gram, *even),
        flops=work,
        name="second_even",
    )
    grown_two, gram_two = call(
        functools.partial(grown_two_kernel, count=count),
        (f32(vectors, width), f32(vectors, vectors)),
        (degree, *spread(evens, odds)),
        name="grown_two",
    )
    return call(
        functools.partial(finish_kernel, count=count),
        f32(vectors, width),
        (grown_two, *total_gram(gram_two)),
        name="finish",
    )


def build_block(block_points, block_squares, column_points, column_squares):
    products = lax.dot_general(
        block_points, column_points, (((0,), (0,)), ((), ())), precision=lax.Precision.HIGHEST
    )
    distance = block_squares[:, None] + column_squares[None, :] - 2.0 * products
    return jnp.exp(-distance / (0.5 * block_points.shape[0]))


def stored_shards(frames, start):
    block_points = lax.all_gather(frames, "col", axis=1, tiled=True)
    column_points = lax.all_gather(frames, "row", axis=1, tiled=True)
    block_squares = jnp.sum(block_points * block_points, axis=0)
    column_squares = jnp.sum(column_points * column_points, axis=0)
    frame_count = frames.shape[1] * lax.axis_size("row") * lax.axis_size("col")
    block_rows = block_points.shape[1]
    height = min(512, block_rows)
    stored = [
        build_block(
            block_points[:, first : first + height],
            block_squares[first : first + height],
            column_points,
            column_squares,
        )
        for first in range(0, block_rows, height)
    ]

    def settle(partial_value):
        return lax.psum_scatter(partial_value, "col", scatter_dimension=1, tiled=True)

    def kernel_product(weights):
        spread_weights = lax.all_gather(weights, "row", axis=1, tiled=True)
        return settle(
            jnp.concatenate([exact(spread_weights, part, ROWS_BY_ROWS) for part in stored], axis=1)
        )

    def orthonormal(vectors):
        gram = lax.psum(exact(vectors, vectors, ROWS_BY_ROWS), ("row", "col")) / frame_count
        return jax.scipy.linalg.solve_triangular(jnp.linalg.cholesky(gram), vectors, lower=True)

    sums = jnp.concatenate([jnp.sum(part, axis=1)[None, :] for part in stored], axis=1)
    inverse = 1.0 / settle(sums)
    degree = kernel_product(inverse)
    basis_one = orthonormal(kernel_product(start * inverse) / degree)
    return orthonormal(kernel_product(basis_one * inverse) / degree)


def shards(frames, start):
    row_size, column_size = lax.axis_size("row"), lax.axis_size("col")
    entries = row_size * column_size * frames.shape[1] ** 2
    powers = row_size & (row_size - 1) == 0 and column_size & (column_size - 1) == 0
    if powers and row_size > 1 and 4 * entries <= RESIDENT_BYTES:
        return resident_shards(frames, start)
    return stored_shards(frames, start)


def solution(mesh):
    return jax.shard_map(
        shards,
        mesh=mesh,
        in_specs=(P(None, ("row", "col")), P(None, ("row", "col"))),
        out_specs=P(None, ("row", "col")),
        check_vma=False,
    )
```

```python
import functools
import math
import jax
import jax.numpy as jnp
from jax import lax
from jax.experimental import pallas as pl
from jax.experimental.pallas import tpu as pltpu
from jax.sharding import PartitionSpec as P

VMEM = pl.BlockSpec(memory_space=pltpu.VMEM)
ROWS_BY_COLUMNS = (((1,), (0,)), ((), ()))
ROWS_BY_ROWS = (((1,), (1,)), ((), ()))
RESIDENT_BYTES = 36 << 20
DEGREE_ROWS = 16


def call(body, out_shape, operands, scratch=(), limit=14 << 20, flops=0, name=None):
    return pl.pallas_call(
        body,
        out_shape=out_shape,
        in_specs=[VMEM] * len(operands),
        out_specs=jax.tree.map(lambda _: VMEM, out_shape),
        scratch_shapes=list(scratch),
        compiler_params=pltpu.CompilerParams(vmem_limit_bytes=limit),
        cost_estimate=pl.CostEstimate(flops=flops, bytes_accessed=0, transcendentals=0) if flops else None,
        name=name,
    )(*operands)


def f32(*shape):
    return jax.ShapeDtypeStruct(shape, jnp.float32)


def bf16(*shape):
    return jax.ShapeDtypeStruct(shape, jnp.bfloat16)


def halves(values):
    high = values.astype(jnp.bfloat16)
    return high, (values - high.astype(jnp.float32)).astype(jnp.bfloat16)


def thirds(values):
    high = values.astype(jnp.bfloat16).astype(jnp.float32)
    middle = (values - high).astype(jnp.bfloat16).astype(jnp.float32)
    return high, middle, values - high - middle


def row_operand(points, left, span):
    width, features = points.shape
    high, low = halves(points)
    left[span, 0:features] = high
    left[span, features : 2 * features] = high
    left[span, 2 * features : 3 * features] = low
    first, second, third = thirds(0.5 * jnp.sum(points * points, axis=1, keepdims=True))
    lane = lax.broadcasted_iota(jnp.int32, (width, features), 1)
    tail = jnp.where(lane == 0, first, jnp.where(lane == 1, second, jnp.where(lane == 2, third, 0.0)))
    tail = jnp.where((lane > 2) & (lane < 6), -1.0, tail)
    left[span, 3 * features : 4 * features] = tail.astype(jnp.bfloat16)


def column_operand(points, right, span):
    features, width = points.shape
    high, low = halves(points)
    right[0:features, span] = high
    right[features : 2 * features, span] = low
    right[2 * features : 3 * features, span] = high
    first, second, third = thirds(0.5 * jnp.sum(points * points, axis=0, keepdims=True))
    line = lax.broadcasted_iota(jnp.int32, (features, width), 0)
    tail = jnp.where(line == 3, first, jnp.where(line == 4, second, jnp.where(line == 5, third, 0.0)))
    tail = jnp.where(line < 3, -1.0, tail)
    right[3 * features : 4 * features, span] = tail.astype(jnp.bfloat16)


def build_rows(left, right, high_ref, low_ref, totals, tile_rows=256, tile_columns=512):
    width = left.shape[0]
    for start in range(0, width, tile_rows):
        lines = slice(start, start + tile_rows)
        points = left[lines, :]
        total = jnp.zeros((tile_rows, 128), jnp.float32)
        for first in range(0, right.shape[1], tile_columns):
            span = slice(first, first + tile_columns)
            values = jnp.exp2(
                lax.dot_general(points, right[:, span], ROWS_BY_COLUMNS, preferred_element_type=jnp.float32)
            )
            high = values.astype(jnp.bfloat16)
            high_ref[lines, span] = high
            low_ref[lines, span] = (values - high.astype(jnp.float32)).astype(jnp.bfloat16)
            for lane in range(0, tile_columns, 128):
                total = total + values[:, lane : lane + 128]
        totals[lines, :] = total
    return jnp.sum(totals[...].T, axis=0, keepdims=True)


def point_scale(features):
    return math.sqrt(math.log2(math.e) / (0.25 * features))


def build_near_kernel(*refs, row_parts, column_parts):
    row_refs, column_refs = refs[:row_parts], (refs[0], *refs[row_parts : row_parts + column_parts - 1])
    outs = refs[row_parts + column_parts - 1 :]
    sums_ref, left_ref, right, totals = outs[2 * row_parts :]
    features, width = row_refs[0].shape
    scale = point_scale(features)
    for part, ref in enumerate(column_refs):
        column_operand(ref[...] * scale, right, slice(part * width, (part + 1) * width))
    for part, (high_ref, low_ref) in enumerate(pairs(outs[: 2 * row_parts])):
        lines = slice(part * width, (part + 1) * width)
        row_operand(row_refs[part][...].T * scale, left_ref, lines)
        sums_ref[part : part + 1, :] = build_rows(left_ref.at[lines, :], right, high_ref, low_ref, totals)
    sums_ref[row_parts:, :] = jnp.zeros((sums_ref.shape[0] - row_parts, width), jnp.float32)


def build_far_kernel(*refs, row_parts, column_parts):
    left_ref, sums_ref, start_ref, column_refs = refs[0], refs[1], refs[2], refs[3 : 3 + column_parts]
    outs = refs[3 + column_parts :]
    packed_ref, right, totals = outs[2 * row_parts :]
    vectors, width = start_ref.shape
    scale = point_scale(column_refs[0].shape[0])
    packed_ref[0:vectors, :] = start_ref[...]
    packed_ref[vectors:, :] = sums_ref[...]
    for part, ref in enumerate(column_refs):
        column_operand(ref[...] * scale, right, slice(part * width, (part + 1) * width))
    for part, (high_ref, low_ref) in enumerate(pairs(outs[: 2 * row_parts])):
        lines = slice(part * width, (part + 1) * width)
        line = vectors + part
        packed_ref[line : line + 1, :] += build_rows(left_ref.at[lines, :], right, high_ref, low_ref, totals)


def sweep(weights, parts, stores, block, initial=None, tile=256):
    rows = weights.shape[0] // 2
    width = stores[0][0].shape[0]
    pieces = []
    for first in range(0, width, tile):
        span = slice(block * width + first, block * width + first + tile)
        total = None if initial is None else initial[:, first : first + tile]
        for part, (high_ref, low_ref) in zip(parts, stores):
            lines = slice(part * width, (part + 1) * width)
            both = lax.dot_general(
                weights[:, lines], high_ref[:, span], ROWS_BY_COLUMNS, preferred_element_type=jnp.float32
            )
            last = lax.dot_general(
                weights[0:rows, lines], low_ref[:, span], ROWS_BY_COLUMNS, preferred_element_type=jnp.float32
            )
            term = both[0:rows] + both[rows:] + last
            total = term if total is None else total + term
        pieces.append(total)
    return jnp.concatenate(pieces, axis=1)


def pairs(refs):
    return list(zip(refs[0::2], refs[1::2]))


def place_of(block, odd):
    return block // 2, block % 2 + (2 if odd else 0)


def halved(refs, parts):
    return pairs(refs[: 2 * parts]), pairs(refs[2 * parts : 4 * parts])


def first_kernel(*refs, parts):
    packed_refs, stores = refs[:parts], halved(refs[parts : 5 * parts], parts)
    out_ref, inverse_ref, weights = refs[5 * parts :]
    rows = weights.shape[0] // 2
    vectors = rows - DEGREE_ROWS
    width = packed_refs[0].shape[1]
    kept = out_ref.shape[1]
    for part in range(parts):
        span = slice(part * width, (part + 1) * width)
        density = packed_refs[0][vectors + part : vectors + part + 1, :]
        for peer in range(1, parts):
            line = vectors + (part ^ peer)
            density = density + packed_refs[peer][line : line + 1, :]
        inverse = 1.0 / density
        if part == 0:
            inverse_ref[...] = inverse
        line = lax.broadcasted_iota(jnp.int32, (DEGREE_ROWS, width), 0)
        for first, piece in (
            (0, packed_refs[part][0:vectors, :] * inverse),
            (vectors, jnp.where(line == 0, inverse, 0.0)),
        ):
            high, low = halves(piece)
            last = first + piece.shape[0]
            weights[first:last, span] = high
            weights[rows + first : rows + last, span] = low
    for block in range(out_ref.shape[0]):
        half, place = place_of(block, True)
        out_ref[block] = sweep(weights, range(parts), stores[half], place)[0:kept]


def far_kernel(*refs, parts):
    weights, stores, out_ref = refs[0], halved(refs[1 : 1 + 4 * parts], parts), refs[-1]
    for index in range(out_ref.shape[0]):
        half, place = place_of(1 + index, False)
        out_ref[index] = sweep(weights, range(parts), stores[half], place)[0 : out_ref.shape[1]]


def own_kernel(*refs, parts):
    weights, stores, out_ref = refs[0], pairs(refs[2 : 2 + 2 * parts]), refs[-1]
    out_ref[...] = sweep(weights, range(parts), stores, 0)[0 : out_ref.shape[0]]


def second_start_kernel(piece_ref, high_ref, low_ref, far_high_ref, far_low_ref, odd_ref, even_ref, weights):
    vectors, width = piece_ref.shape[0], high_ref.shape[0]
    high, low = halves(piece_ref[:, 0:width])
    weights[0:vectors, :] = high
    weights[vectors:, :] = low
    stores = (high_ref, low_ref), (far_high_ref, far_low_ref)
    for odd, out_ref in ((True, odd_ref), (False, even_ref)):
        for block in range(out_ref.shape[0]):
            half, place = place_of(block, odd)
            out_ref[block] = sweep(weights, (0,), [stores[half]], place)


def second_odd_kernel(*refs, parts):
    piece_refs, partial_ref = refs[: 1 + parts], refs[1 + parts]
    stores = halved(refs[2 + parts : 2 + 5 * parts], parts)
    out_ref, gram_ref, weights = refs[2 + 5 * parts :]
    vectors, width = piece_refs[0].shape[0], stores[0][0][0].shape[0]
    gram = piece_refs[0][:, width:]
    for part, ref in enumerate(piece_refs[1:]):
        gram = gram + ref[:, width:]
        span = slice(part * width, (part + 1) * width)
        high, low = halves(ref[:, 0:width])
        weights[0:vectors, span] = high
        weights[vectors:, span] = low
    gram_ref[...] = gram
    for block in range(out_ref.shape[0]):
        half, place = place_of(block, True)
        out_ref[block, :, 0:width] = sweep(weights, range(parts), stores[half], place, partial_ref[block])
        out_ref[block, :, width:] = gram


def second_even_kernel(*refs, parts):
    weights, gram_ref, partial_ref = refs[:3]
    stores, out_ref = halved(refs[3 : 3 + 4 * parts], parts), refs[-1]
    width = stores[0][0][0].shape[0]
    for index in range(out_ref.shape[0]):
        half, place = place_of(1 + index, False)
        out_ref[index, :, 0:width] = sweep(
            weights, range(parts), stores[half], place, partial_ref[1 + index]
        )
        out_ref[index, :, width:] = gram_ref[...]


def second_own_kernel(*refs, parts):
    weights, gram_ref, partial_ref = refs[:3]
    stores, out_ref = pairs(refs[4 : 4 + 2 * parts]), refs[-1]
    width = stores[0][0].shape[0]
    out_ref[:, 0:width] = sweep(weights, range(parts), stores, 0, partial_ref[0])
    out_ref[:, width:] = gram_ref[...]


def exact(left, right, dims):
    return lax.dot_general(
        left, right, dims, precision=lax.Precision.HIGHEST, preferred_element_type=jnp.float32
    )


def grown_kernel(*refs):
    inverse_ref, piece_refs, (grown_ref, degree_ref) = refs[0], refs[1:-2], refs[-2:]
    vectors = grown_ref.shape[0]
    width = degree_ref.shape[1]
    total = piece_refs[0][...]
    for ref in piece_refs[1:]:
        total = total + ref[...]
    degree = total[vectors : vectors + 1, :]
    grown = total[0:vectors, :] / degree
    degree_ref[...] = degree
    grown_ref[:, 0:width] = grown * inverse_ref[...]
    gram = exact(grown, grown, ROWS_BY_ROWS)
    grown_ref[:, width:] = jnp.concatenate([gram, jnp.zeros((vectors, 128 - vectors), jnp.float32)], axis=1)


def inverse_factor(gram, panel=16):
    size = gram.shape[0]
    shape = (size, 2 * size)
    line = lax.broadcasted_iota(jnp.int32, (size, size), 0)
    lane = lax.broadcasted_iota(jnp.int32, (size, size), 1)
    table = jnp.concatenate([gram, jnp.where(line == lane, 1.0, 0.0)], axis=1)
    tall = lax.broadcasted_iota(jnp.int32, shape, 0)
    pivots = jnp.zeros(shape, jnp.float32)
    for first in range(0, size, panel):
        columns = [jnp.broadcast_to(table[:, step : step + 1], shape) for step in range(first, first + panel)]
        for place, step in enumerate(range(first, first + panel)):
            pivot = columns[place][step : step + 1, :]
            pivots = jnp.where(tall == step, pivot, pivots)
            factor = jnp.where(tall > step, columns[place] * (1.0 / pivot), 0.0)
            for later in range(place + 1, panel):
                columns[later] = columns[later] - factor * columns[later][step : step + 1, :]
            table = table - factor * table[step : step + 1, :]
    return table[:, size:] * lax.rsqrt(pivots[:, size:])


def grown_two_kernel(*refs, count):
    degree_ref, piece_refs, (grown_ref, gram_ref) = refs[0], refs[1:-2], refs[-2:]
    vectors, width = grown_ref.shape
    total = piece_refs[0][...]
    for ref in piece_refs[1:]:
        total = total + ref[...]
    factor = inverse_factor(total[:, width : width + vectors] * (1.0 / count))
    grown = exact(factor, total[:, 0:width] / degree_ref[...], ROWS_BY_COLUMNS)
    grown_ref[...] = grown
    gram_ref[...] = exact(grown, grown, ROWS_BY_ROWS)


def finish_kernel(*refs, count):
    grown_ref, gram_refs, out_ref = refs[0], refs[1:-1], refs[-1]
    gram = gram_refs[0][...]
    for ref in gram_refs[1:]:
        gram = gram + ref[...]
    out_ref[...] = exact(inverse_factor(gram * (1.0 / count)), grown_ref[...], ROWS_BY_COLUMNS)


def swap(values, mask):
    size = lax.axis_size(("row", "col"))
    return lax.ppermute(values, ("row", "col"), [(index, index ^ mask) for index in range(size)])


def resident_shards(frames, start):
    row_size, column_size = lax.axis_size("row"), lax.axis_size("col")
    count = frames.shape[1] * row_size * column_size
    features, width = frames.shape
    vectors = start.shape[0]

    core, across, along, skip = column_size, column_size * row_size // 2, 1, column_size // 2
    beside = 2 * core
    near = (along, across, along | across)
    far = (beside, skip, skip | beside)
    parts, half = 4, 4

    skip_piece = swap(frames, skip)
    beside_piece = swap(frames, beside)
    row_pieces = [frames] + [swap(frames, mask) for mask in near]
    both_piece = swap(skip_piece, beside)
    near_columns = [beside_piece, swap(frames, core), swap(beside_piece, core)]
    far_columns = [skip_piece, both_piece, swap(skip_piece, core), swap(both_piece, core)]

    operands = 4 * features
    columns = half * width
    stored = (bf16(width, columns),) * (2 * parts)
    totals = pltpu.VMEM((width, 128), jnp.float32)
    *near_store, sums, left = call(
        functools.partial(build_near_kernel, row_parts=parts, column_parts=half),
        (*stored, f32(8, width), bf16(parts * width, operands)),
        (*row_pieces, *near_columns),
        scratch=(pltpu.VMEM((operands, columns), jnp.bfloat16), totals),
        flops=1,
        name="build_near",
    )
    *far_store, packed = call(
        functools.partial(build_far_kernel, row_parts=parts, column_parts=half),
        (*stored, f32(vectors + 8, width)),
        (left, sums, start, *far_columns),
        scratch=(pltpu.VMEM((operands, columns), jnp.bfloat16), totals),
        flops=1,
        name="build_far",
    )
    all_packed = [packed] + [swap(packed, mask) for mask in near]

    def spread(odds, evens):
        odds = swap(odds, core)
        both = evens + odds[1:]
        return odds[0], both, [swap(both[place], mask) for place, mask in enumerate(far)]

    def total_gram(gram):
        gram = gram + swap(gram, core)
        gram = functools.reduce(jnp.add, [swap(gram, mask) for mask in near], gram)
        return [gram] + [swap(gram, mask) for mask in far]

    rows = vectors + DEGREE_ROWS
    block = 2 * 3 * rows * parts * width * width
    odds, inverse, weights = call(
        functools.partial(first_kernel, parts=parts),
        (f32(half, vectors + 8, width), f32(1, width), bf16(2 * rows, parts * width)),
        (*all_packed, *near_store, *far_store),
        flops=half * block,
        name="first_odd",
    )
    evens = call(
        functools.partial(far_kernel, parts=parts),
        f32(half - 1, vectors + 8, width),
        (weights, *near_store, *far_store),
        flops=(half - 1) * block,
        name="first_even",
    )
    own_odd, both, others = spread(odds, evens)
    own_even = call(
        functools.partial(own_kernel, parts=parts),
        f32(vectors + 8, width),
        (weights, both, *near_store),
        flops=block,
        name="first_own",
    )
    weighted, degree = call(
        grown_kernel,
        (f32(vectors, width + 128), f32(1, width)),
        (inverse, own_even, own_odd, *others),
        name="grown",
    )
    pieces = [weighted] + [swap(weighted, mask) for mask in near]
    odd_partial, even_partial = call(
        second_start_kernel,
        (f32(half, vectors, width),) * 2,
        (weighted, *near_store[0:2], *far_store[0:2]),
        scratch=(pltpu.VMEM((2 * vectors, width), jnp.bfloat16),),
        flops=2 * half * block // parts,
        name="second_start",
    )
    rest = parts - 1
    odds, gram, weights = call(
        functools.partial(second_odd_kernel, parts=rest),
        (f32(half, vectors, width + 128), f32(vectors, 128), bf16(2 * vectors, rest * width)),
        (*pieces, odd_partial, *near_store[2:], *far_store[2:]),
        flops=half * block,
        name="second_odd",
    )
    evens = call(
        functools.partial(second_even_kernel, parts=rest),
        f32(half - 1, vectors, width + 128),
        (weights, gram, even_partial, *near_store[2:], *far_store[2:]),
        flops=(half - 1) * block,
        name="second_even",
    )
    own_odd, both, others = spread(odds, evens)
    own_even = call(
        functools.partial(second_own_kernel, parts=rest),
        f32(vectors, width + 128),
        (weights, gram, even_partial, both, *near_store[2:]),
        flops=block,
        name="second_own",
    )
    grown_two, gram_two = call(
        functools.partial(grown_two_kernel, count=count),
        (f32(vectors, width), f32(vectors, vectors)),
        (degree, own_even, own_odd, *others),
        name="grown_two",
    )
    return call(
        functools.partial(finish_kernel, count=count),
        f32(vectors, width),
        (grown_two, *total_gram(gram_two)),
        name="finish",
    )


def build_block(block_points, block_squares, column_points, column_squares):
    products = lax.dot_general(
        block_points, column_points, (((0,), (0,)), ((), ())), precision=lax.Precision.HIGHEST
    )
    distance = block_squares[:, None] + column_squares[None, :] - 2.0 * products
    return jnp.exp(-distance / (0.5 * block_points.shape[0]))


def stored_shards(frames, start):
    block_points = lax.all_gather(frames, "col", axis=1, tiled=True)
    column_points = lax.all_gather(frames, "row", axis=1, tiled=True)
    block_squares = jnp.sum(block_points * block_points, axis=0)
    column_squares = jnp.sum(column_points * column_points, axis=0)
    frame_count = frames.shape[1] * lax.axis_size("row") * lax.axis_size("col")
    block_rows = block_points.shape[1]
    height = min(512, block_rows)
    stored = [
        build_block(
            block_points[:, first : first + height],
            block_squares[first : first + height],
            column_points,
            column_squares,
        )
        for first in range(0, block_rows, height)
    ]

    def settle(partial_value):
        return lax.psum_scatter(partial_value, "col", scatter_dimension=1, tiled=True)

    def kernel_product(weights):
        spread_weights = lax.all_gather(weights, "row", axis=1, tiled=True)
        return settle(
            jnp.concatenate([exact(spread_weights, part, ROWS_BY_ROWS) for part in stored], axis=1)
        )

    def orthonormal(vectors):
        gram = lax.psum(exact(vectors, vectors, ROWS_BY_ROWS), ("row", "col")) / frame_count
        return jax.scipy.linalg.solve_triangular(jnp.linalg.cholesky(gram), vectors, lower=True)

    sums = jnp.concatenate([jnp.sum(part, axis=1)[None, :] for part in stored], axis=1)
    inverse = 1.0 / settle(sums)
    degree = kernel_product(inverse)
    basis_one = orthonormal(kernel_product(start * inverse) / degree)
    return orthonormal(kernel_product(basis_one * inverse) / degree)


def shards(frames, start):
    row_size, column_size = lax.axis_size("row"), lax.axis_size("col")
    entries = row_size * column_size * frames.shape[1] ** 2
    if (row_size, column_size) == (8, 4) and 4 * entries <= RESIDENT_BYTES:
        return resident_shards(frames, start)
    return stored_shards(frames, start)


def solution(mesh):
    return jax.shard_map(
        shards,
        mesh=mesh,
        in_specs=(P(None, ("row", "col")), P(None, ("row", "col"))),
        out_specs=P(None, ("row", "col")),
        check_vma=False,
    )
```

```python
import functools
import math
import jax
import jax.numpy as jnp
from jax import lax
from jax.experimental import pallas as pl
from jax.experimental.pallas import tpu as pltpu
from jax.sharding import PartitionSpec as P

VMEM = pl.BlockSpec(memory_space=pltpu.VMEM)
ROWS_BY_COLUMNS = (((1,), (0,)), ((), ()))
ROWS_BY_ROWS = (((1,), (1,)), ((), ()))
RESIDENT_BYTES = 36 << 20
DEGREE_ROWS = 16


def call(body, out_shape, operands, scratch=(), limit=14 << 20, flops=0, name=None):
    return pl.pallas_call(
        body,
        out_shape=out_shape,
        in_specs=[VMEM] * len(operands),
        out_specs=jax.tree.map(lambda _: VMEM, out_shape),
        scratch_shapes=list(scratch),
        compiler_params=pltpu.CompilerParams(vmem_limit_bytes=limit),
        cost_estimate=pl.CostEstimate(flops=flops, bytes_accessed=0, transcendentals=0) if flops else None,
        name=name,
    )(*operands)


def f32(*shape):
    return jax.ShapeDtypeStruct(shape, jnp.float32)


def bf16(*shape):
    return jax.ShapeDtypeStruct(shape, jnp.bfloat16)


def halves(values):
    high = values.astype(jnp.bfloat16)
    return high, (values - high.astype(jnp.float32)).astype(jnp.bfloat16)


def thirds(values):
    high = values.astype(jnp.bfloat16).astype(jnp.float32)
    middle = (values - high).astype(jnp.bfloat16).astype(jnp.float32)
    return high, middle, values - high - middle


def pack(values):
    return jnp.concatenate([values[:, first : first + 128] for first in range(0, values.shape[1], 128)], axis=0)


def unpack(packed, lines, width):
    count = width // 128
    return jnp.concatenate([packed[block * lines : (block + 1) * lines] for block in range(count)], axis=1)


def pack_square(square):
    lines = square.shape[0] * square.shape[0] // 128
    return jnp.concatenate([square[first : first + lines] for first in range(0, square.shape[0], lines)], axis=1)


def unpack_square(packed, size):
    return jnp.concatenate([packed[:, first : first + size] for first in range(0, packed.shape[1], size)], axis=0)


def row_operand(points, left, span):
    width, features = points.shape
    high, low = halves(points)
    left[span, 0:features] = high
    left[span, features : 2 * features] = high
    left[span, 2 * features : 3 * features] = low
    first, second, third = thirds(0.5 * jnp.sum(points * points, axis=1, keepdims=True))
    lane = lax.broadcasted_iota(jnp.int32, (width, features), 1)
    tail = jnp.where(lane == 0, first, jnp.where(lane == 1, second, jnp.where(lane == 2, third, 0.0)))
    tail = jnp.where((lane > 2) & (lane < 6), -1.0, tail)
    left[span, 3 * features : 4 * features] = tail.astype(jnp.bfloat16)


def column_operand(points, right, span):
    features, width = points.shape
    high, low = halves(points)
    right[0:features, span] = high
    right[features : 2 * features, span] = low
    right[2 * features : 3 * features, span] = high
    first, second, third = thirds(0.5 * jnp.sum(points * points, axis=0, keepdims=True))
    line = lax.broadcasted_iota(jnp.int32, (features, width), 0)
    tail = jnp.where(line == 3, first, jnp.where(line == 4, second, jnp.where(line == 5, third, 0.0)))
    tail = jnp.where(line < 3, -1.0, tail)
    right[3 * features : 4 * features, span] = tail.astype(jnp.bfloat16)


def build_rows(left, right, high_ref, low_ref, totals, tile_rows=256, tile_columns=512):
    width = left.shape[0]
    for start in range(0, width, tile_rows):
        lines = slice(start, start + tile_rows)
        points = left[lines, :]
        total = jnp.zeros((tile_rows, 128), jnp.float32)
        for first in range(0, right.shape[1], tile_columns):
            span = slice(first, first + tile_columns)
            values = jnp.exp2(
                lax.dot_general(points, right[:, span], ROWS_BY_COLUMNS, preferred_element_type=jnp.float32)
            )
            high = values.astype(jnp.bfloat16)
            high_ref[lines, span] = high
            low_ref[lines, span] = (values - high.astype(jnp.float32)).astype(jnp.bfloat16)
            for lane in range(0, tile_columns, 128):
                total = total + values[:, lane : lane + 128]
        totals[lines, :] = total
    return jnp.sum(totals[...].T, axis=0, keepdims=True)


def point_scale(features):
    return math.sqrt(math.log2(math.e) / (0.25 * features))


def build_near_kernel(*refs, row_parts, column_parts):
    row_refs, column_refs = refs[:row_parts], (refs[0], *refs[row_parts : row_parts + column_parts - 1])
    outs = refs[row_parts + column_parts - 1 :]
    sums_ref, left_ref, right, totals = outs[2 * row_parts :]
    features, width = row_refs[0].shape
    scale = point_scale(features)
    for part, ref in enumerate(column_refs):
        column_operand(ref[...] * scale, right, slice(part * width, (part + 1) * width))
    sums_ref[...] = jnp.zeros_like(sums_ref)
    for part, (high_ref, low_ref) in enumerate(pairs(outs[: 2 * row_parts])):
        lines = slice(part * width, (part + 1) * width)
        row_operand(row_refs[part][...].T * scale, left_ref, lines)
        sums_ref[part : part + 1, :] = build_rows(left_ref.at[lines, :], right, high_ref, low_ref, totals)


def build_far_kernel(*refs, row_parts, column_parts):
    left_ref, near_right, near_sums_ref, start_ref, last_ref = refs[:5]
    column_refs, outs = refs[5 : 5 + column_parts], refs[5 + column_parts :]
    packed_ref, right, left, totals = outs[2 * row_parts + 4 :]
    vectors, width = start_ref.shape
    lanes = width // 128
    scale = point_scale(last_ref.shape[0])
    packed_ref[0 : vectors * lanes, :] = pack(start_ref[...])
    for part, ref in enumerate(column_refs):
        column_operand(ref[...] * scale, right, slice(part * width, (part + 1) * width))
    stores = pairs(outs[: 2 * row_parts + 4])

    def put(part, sums):
        line = (vectors + part) * lanes
        packed_ref[line : line + lanes, :] = pack(sums)

    for part in range(row_parts):
        lines = slice(part * width, (part + 1) * width)
        sums = build_rows(left_ref.at[lines, :], right, *stores[part], totals)
        put(part, near_sums_ref[part : part + 1, :] + sums)
    row_operand(last_ref[...].T * scale, left, slice(0, width))
    sums = build_rows(left, near_right, *stores[row_parts], totals)
    put(row_parts, sums + build_rows(left, right, *stores[row_parts + 1], totals))


def sweep(weights, parts, stores, block, initial=None, tile=256):
    rows = weights.shape[0] // 2
    width = stores[0][0].shape[0]
    pieces = []
    for first in range(0, width, tile):
        span = slice(block * width + first, block * width + first + tile)
        total = None if initial is None else initial[:, first : first + tile]
        for part, (high_ref, low_ref) in zip(parts, stores):
            lines = slice(part * width, (part + 1) * width)
            both = lax.dot_general(
                weights[:, lines], high_ref[:, span], ROWS_BY_COLUMNS, preferred_element_type=jnp.float32
            )
            last = lax.dot_general(
                weights[0:rows, lines], low_ref[:, span], ROWS_BY_COLUMNS, preferred_element_type=jnp.float32
            )
            term = both[0:rows] + both[rows:] + last
            total = term if total is None else total + term
        pieces.append(total)
    return jnp.concatenate(pieces, axis=1)


def pairs(refs):
    return list(zip(refs[0::2], refs[1::2]))


def place_of(block, odd):
    return block // 2, block % 2 + (2 if odd else 0)


def halved(refs, parts):
    return pairs(refs[: 2 * parts]), pairs(refs[2 * parts : 4 * parts])


def put_product(out_ref, product, vectors):
    width = product.shape[1]
    lanes = width // 128
    last = vectors * lanes
    out_ref[0:last, :] = pack(product[0:vectors])
    out_ref[last : last + 8, :] = jnp.zeros((8, 128), jnp.float32)
    out_ref[last : last + lanes, :] = pack(product[vectors : vectors + 1])


def first_kernel(*refs, parts):
    packed_refs, stores = refs[:parts], halved(refs[parts : 5 * parts], parts)
    out_ref, inverse_ref, weights = refs[5 * parts :]
    rows = weights.shape[0] // 2
    vectors = rows - DEGREE_ROWS
    width = inverse_ref.shape[1]
    lanes = width // 128

    def sums(peer, part):
        line = (vectors + part) * lanes
        return unpack(packed_refs[peer][line : line + lanes, :], 1, width)

    for part in range(parts):
        span = slice(part * width, (part + 1) * width)
        density = sums(0, part)
        for peer in range(1, parts):
            density = density + sums(peer, part ^ peer)
        inverse = 1.0 / density
        if part == 0:
            inverse_ref[...] = inverse
        line = lax.broadcasted_iota(jnp.int32, (DEGREE_ROWS, width), 0)
        for first, piece in (
            (0, unpack(packed_refs[part][0 : vectors * lanes, :], vectors, width) * inverse),
            (vectors, jnp.where(line == 0, inverse, 0.0)),
        ):
            high, low = halves(piece)
            last = first + piece.shape[0]
            weights[first:last, span] = high
            weights[rows + first : rows + last, span] = low
    for block in range(out_ref.shape[0]):
        half, place = place_of(block, True)
        put_product(out_ref.at[block], sweep(weights, range(parts), stores[half], place), vectors)


def far_kernel(*refs, parts, vectors):
    weights, stores, out_ref = refs[0], halved(refs[1 : 1 + 4 * parts], parts), refs[-1]
    for index in range(out_ref.shape[0]):
        half, place = place_of(1 + index, False)
        put_product(out_ref.at[index], sweep(weights, range(parts), stores[half], place), vectors)


def own_kernel(*refs, parts, vectors):
    weights, stores, out_ref = refs[0], pairs(refs[2 : 2 + 2 * parts]), refs[-1]
    put_product(out_ref, sweep(weights, range(parts), stores, 0), vectors)


def put_weights(weights, packed, place):
    vectors = weights.shape[0] // 2
    width = weights.shape[1] if place is None else packed.shape[0] // vectors * 128
    values = unpack(packed[0 : vectors * (width // 128), :], vectors, width)
    span = slice(0, width) if place is None else slice(place * width, (place + 1) * width)
    high, low = halves(values)
    weights[0:vectors, span] = high
    weights[vectors:, span] = low


def second_part_kernel(piece_ref, *refs):
    stores, (odd_ref, even_ref, weights) = pairs(refs[0:4]), refs[-3:]
    earlier = refs[4:-3] or (None, None)
    put_weights(weights, piece_ref[...], None)
    for odd, earlier_ref, out_ref in ((True, earlier[0], odd_ref), (False, earlier[1], even_ref)):
        for block in range(out_ref.shape[0]):
            half, place = place_of(block, odd)
            initial = None if earlier_ref is None else earlier_ref[block]
            out_ref[block] = sweep(weights, (0,), [stores[half]], place, initial)


def put_second(out_ref, product, gram):
    last = out_ref.shape[0] - gram.shape[0]
    out_ref[0:last, :] = pack(product)
    out_ref[last:, :] = gram


def second_odd_kernel(*refs, parts):
    piece_refs, refs = refs[:4], refs[4:]
    partial_ref, stores = refs[0], halved(refs[1 : 1 + 4 * parts], parts)
    out_ref, gram_ref, weights = refs[1 + 4 * parts :]
    last = piece_refs[0].shape[0] - gram_ref.shape[0]
    gram = piece_refs[0][last:, :]
    for ref in piece_refs[1:]:
        gram = gram + ref[last:, :]
    gram_ref[...] = gram
    for part, ref in enumerate(piece_refs[-parts:]):
        put_weights(weights, ref[...], part)
    for block in range(out_ref.shape[0]):
        half, place = place_of(block, True)
        product = sweep(weights, range(parts), stores[half], place, partial_ref[block])
        put_second(out_ref.at[block], product, gram)


def second_even_kernel(*refs, parts):
    weights, gram_ref, partial_ref = refs[:3]
    stores, out_ref = halved(refs[3 : 3 + 4 * parts], parts), refs[-1]
    for index in range(out_ref.shape[0]):
        half, place = place_of(1 + index, False)
        product = sweep(weights, range(parts), stores[half], place, partial_ref[1 + index])
        put_second(out_ref.at[index], product, gram_ref[...])


def second_own_kernel(*refs, parts):
    weights, gram_ref, partial_ref = refs[:3]
    stores, out_ref = pairs(refs[4 : 4 + 2 * parts]), refs[-1]
    put_second(out_ref, sweep(weights, range(parts), stores, 0, partial_ref[0]), gram_ref[...])


def exact(left, right, dims):
    return lax.dot_general(
        left, right, dims, precision=lax.Precision.HIGHEST, preferred_element_type=jnp.float32
    )


def add_up(refs):
    total = refs[0][...]
    for ref in refs[1:]:
        total = total + ref[...]
    return total


def grown_kernel(*refs):
    inverse_ref, piece_refs, (grown_ref, degree_ref) = refs[0], refs[1:-2], refs[-2:]
    width = degree_ref.shape[1]
    lanes = width // 128
    vectors = (grown_ref.shape[0] - 8) // lanes
    total = add_up(piece_refs)
    last = vectors * lanes
    degree = unpack(total[last : last + lanes], 1, width)
    grown = unpack(total[0:last], vectors, width) / degree
    degree_ref[...] = degree
    grown_ref[0:last, :] = pack(grown * inverse_ref[...])
    grown_ref[last:, :] = pack_square(exact(grown, grown, ROWS_BY_ROWS))


def inverse_factor(gram, panel=16):
    size = gram.shape[0]
    shape = (size, 2 * size)
    line = lax.broadcasted_iota(jnp.int32, (size, size), 0)
    lane = lax.broadcasted_iota(jnp.int32, (size, size), 1)
    table = jnp.concatenate([gram, jnp.where(line == lane, 1.0, 0.0)], axis=1)
    tall = lax.broadcasted_iota(jnp.int32, shape, 0)
    pivots = jnp.zeros(shape, jnp.float32)
    for first in range(0, size, panel):
        columns = [jnp.broadcast_to(table[:, step : step + 1], shape) for step in range(first, first + panel)]
        for place, step in enumerate(range(first, first + panel)):
            pivot = columns[place][step : step + 1, :]
            pivots = jnp.where(tall == step, pivot, pivots)
            factor = jnp.where(tall > step, columns[place] * (1.0 / pivot), 0.0)
            for later in range(place + 1, panel):
                columns[later] = columns[later] - factor * columns[later][step : step + 1, :]
            table = table - factor * table[step : step + 1, :]
    return table[:, size:] * lax.rsqrt(pivots[:, size:])


def grown_two_kernel(*refs, count):
    degree_ref, piece_refs, (grown_ref, gram_ref) = refs[0], refs[1:-2], refs[-2:]
    vectors, width = grown_ref.shape
    total = add_up(piece_refs)
    last = vectors * (width // 128)
    factor = inverse_factor(unpack_square(total[last:], vectors) * (1.0 / count))
    product = unpack(total[0:last], vectors, width)
    grown = exact(factor, product / degree_ref[...], ROWS_BY_COLUMNS)
    grown_ref[...] = grown
    gram_ref[...] = pack_square(exact(grown, grown, ROWS_BY_ROWS))


def finish_kernel(*refs, count):
    grown_ref, gram_refs, out_ref = refs[0], refs[1:-1], refs[-1]
    gram = unpack_square(add_up(gram_refs), grown_ref.shape[0])
    out_ref[...] = exact(inverse_factor(gram * (1.0 / count)), grown_ref[...], ROWS_BY_COLUMNS)


def swap(values, mask):
    size = lax.axis_size(("row", "col"))
    return lax.ppermute(values, ("row", "col"), [(index, index ^ mask) for index in range(size)])


def fetch_kernel(frames_ref, start_ref, own_ref, own_start_ref, sems):
    copies = [
        pltpu.make_async_copy(source, target, sems.at[index])
        for index, (source, target) in enumerate(((frames_ref, own_ref), (start_ref, own_start_ref)))
    ]
    for copy in copies:
        copy.start()
    for copy in copies:
        copy.wait()


def fetch(frames, start):
    return pl.pallas_call(
        fetch_kernel,
        out_shape=(f32(*frames.shape), f32(*start.shape)),
        in_specs=[pl.BlockSpec(memory_space=pltpu.HBM)] * 2,
        out_specs=(VMEM, VMEM),
        scratch_shapes=[pltpu.SemaphoreType.DMA((2,))],
        compiler_params=pltpu.CompilerParams(vmem_limit_bytes=1 << 20),
        cost_estimate=pl.CostEstimate(flops=1 << 34, bytes_accessed=0, transcendentals=0),
        name="fetch",
    )(pltpu.with_memory_space_constraint(frames, pltpu.HBM), pltpu.with_memory_space_constraint(start, pltpu.HBM))


def resident_shards(frames, start):
    row_size, column_size = lax.axis_size("row"), lax.axis_size("col")
    count = frames.shape[1] * row_size * column_size
    features, width = frames.shape
    vectors = start.shape[0]

    core, across, skip = column_size, column_size * row_size // 2, column_size // 2
    beside, along = 2 * core, 1
    near = (across, skip, across | skip)
    far = (beside, along, beside | along)
    parts, half = 4, 4

    skip_piece = swap(frames, skip)
    own, own_start = fetch(frames, start)
    beside_piece = swap(own, beside)
    along_piece = swap(own, along)
    across_piece = swap(own, across)
    corner_piece = swap(along_piece, beside)
    row_pieces = [across_piece, skip_piece]
    last_piece = swap(skip_piece, across)
    near_columns = [beside_piece, swap(own, core), swap(beside_piece, core)]
    far_columns = [along_piece, corner_piece, swap(along_piece, core), swap(corner_piece, core)]

    operands = 4 * features
    columns = half * width
    lanes = width // 128
    packed_lines = vectors * lanes + 8
    rest = parts - 1
    stored = (bf16(width, columns),) * 2
    totals = pltpu.VMEM((width, 128), jnp.float32)
    *near_store, sums, left, right = call(
        functools.partial(build_near_kernel, row_parts=rest, column_parts=half),
        (*(stored * rest), f32(8, width), bf16(rest * width, operands), bf16(operands, columns)),
        (own, *row_pieces, *near_columns),
        scratch=(totals,),
        flops=1,
        name="build_near",
    )
    *far_store, last_high, last_low, far_high, far_low, packed = call(
        functools.partial(build_far_kernel, row_parts=rest, column_parts=half),
        (*(stored * (rest + 2)), f32((vectors + parts) * lanes, 128)),
        (left, right, sums, own_start, last_piece, *far_columns),
        scratch=(
            pltpu.VMEM((operands, columns), jnp.bfloat16),
            pltpu.VMEM((width, operands), jnp.bfloat16),
            totals,
        ),
        flops=1,
        name="build_far",
    )
    near_store = (*near_store, last_high, last_low)
    far_store = (*far_store, far_high, far_low)
    all_packed = [packed] + [swap(packed, mask) for mask in near]

    def spread(odds, evens):
        odds = swap(odds, core)
        both = evens + odds[1:]
        return odds[0], both, [swap(both[place], mask) for place, mask in enumerate(far)]

    def total_gram(gram):
        gram = gram + swap(gram, core)
        gram = functools.reduce(jnp.add, [swap(gram, mask) for mask in far], gram)
        return [gram] + [swap(gram, mask) for mask in near]

    rows = vectors + DEGREE_ROWS
    block = 2 * 3 * rows * parts * width * width
    odds, inverse, weights = call(
        functools.partial(first_kernel, parts=parts),
        (f32(half, packed_lines, 128), f32(1, width), bf16(2 * rows, parts * width)),
        (*all_packed, *near_store, *far_store),
        flops=half * block,
        name="first_odd",
    )
    evens = call(
        functools.partial(far_kernel, parts=parts, vectors=vectors),
        f32(half - 1, packed_lines, 128),
        (weights, *near_store, *far_store),
        flops=(half - 1) * block,
        name="first_even",
    )
    own_odd, both, others = spread(odds, evens)
    own_even = call(
        functools.partial(own_kernel, parts=parts, vectors=vectors),
        f32(packed_lines, 128),
        (weights, both, *near_store),
        flops=block,
        name="first_own",
    )
    weighted, degree = call(
        grown_kernel,
        (f32(packed_lines, 128), f32(1, width)),
        (inverse, own_even, own_odd, *others),
        name="grown",
    )
    pieces = [weighted] + [swap(weighted, mask) for mask in near]
    partial = ()
    for part in range(2):
        partial = call(
            second_part_kernel,
            (f32(half, vectors, width),) * 2,
            (pieces[part], *near_store[2 * part : 2 * part + 2], *far_store[2 * part : 2 * part + 2], *partial),
            scratch=(pltpu.VMEM((2 * vectors, width), jnp.bfloat16),),
            flops=2 * half * block // parts,
            name="second_part",
        )
    odd_partial, even_partial = partial
    rest = parts - 2
    near_store, far_store = near_store[4:], far_store[4:]
    odds, gram, weights = call(
        functools.partial(second_odd_kernel, parts=rest),
        (f32(half, packed_lines, 128), f32(8, 128), bf16(2 * vectors, rest * width)),
        (*pieces, odd_partial, *near_store, *far_store),
        flops=half * block,
        name="second_odd",
    )
    evens = call(
        functools.partial(second_even_kernel, parts=rest),
        f32(half - 1, packed_lines, 128),
        (weights, gram, even_partial, *near_store, *far_store),
        flops=(half - 1) * block,
        name="second_even",
    )
    own_odd, both, others = spread(odds, evens)
    own_even = call(
        functools.partial(second_own_kernel, parts=rest),
        f32(packed_lines, 128),
        (weights, gram, even_partial, both, *near_store),
        flops=block,
        name="second_own",
    )
    grown_two, gram_two = call(
        functools.partial(grown_two_kernel, count=count),
        (f32(vectors, width), f32(8, 128)),
        (degree, own_even, own_odd, *others),
        name="grown_two",
    )
    return call(
        functools.partial(finish_kernel, count=count),
        f32(vectors, width),
        (grown_two, *total_gram(gram_two)),
        name="finish",
    )


def build_block(block_points, block_squares, column_points, column_squares):
    products = lax.dot_general(
        block_points, column_points, (((0,), (0,)), ((), ())), precision=lax.Precision.HIGHEST
    )
    distance = block_squares[:, None] + column_squares[None, :] - 2.0 * products
    return jnp.exp(-distance / (0.5 * block_points.shape[0]))


def stored_shards(frames, start):
    block_points = lax.all_gather(frames, "col", axis=1, tiled=True)
    column_points = lax.all_gather(frames, "row", axis=1, tiled=True)
    block_squares = jnp.sum(block_points * block_points, axis=0)
    column_squares = jnp.sum(column_points * column_points, axis=0)
    frame_count = frames.shape[1] * lax.axis_size("row") * lax.axis_size("col")
    block_rows = block_points.shape[1]
    height = min(512, block_rows)
    stored = [
        build_block(
            block_points[:, first : first + height],
            block_squares[first : first + height],
            column_points,
            column_squares,
        )
        for first in range(0, block_rows, height)
    ]

    def settle(partial_value):
        return lax.psum_scatter(partial_value, "col", scatter_dimension=1, tiled=True)

    def kernel_product(weights):
        spread_weights = lax.all_gather(weights, "row", axis=1, tiled=True)
        return settle(
            jnp.concatenate([exact(spread_weights, part, ROWS_BY_ROWS) for part in stored], axis=1)
        )

    def orthonormal(vectors):
        gram = lax.psum(exact(vectors, vectors, ROWS_BY_ROWS), ("row", "col")) / frame_count
        return jax.scipy.linalg.solve_triangular(jnp.linalg.cholesky(gram), vectors, lower=True)

    sums = jnp.concatenate([jnp.sum(part, axis=1)[None, :] for part in stored], axis=1)
    inverse = 1.0 / settle(sums)
    degree = kernel_product(inverse)
    basis_one = orthonormal(kernel_product(start * inverse) / degree)
    return orthonormal(kernel_product(basis_one * inverse) / degree)


def shards(frames, start):
    row_size, column_size = lax.axis_size("row"), lax.axis_size("col")
    entries = row_size * column_size * frames.shape[1] ** 2
    shapes = (row_size, column_size, start.shape[0], frames.shape[1] % 128)
    if shapes == (8, 4, 32, 0) and 4 * entries <= RESIDENT_BYTES:
        return resident_shards(frames, start)
    return stored_shards(frames, start)


def solution(mesh):
    return jax.shard_map(
        shards,
        mesh=mesh,
        in_specs=(P(None, ("row", "col")), P(None, ("row", "col"))),
        out_specs=P(None, ("row", "col")),
        check_vma=False,
    )
```

```python
import functools
import math
import jax
import jax.numpy as jnp
from jax import lax
from jax.experimental import pallas as pl
from jax.experimental.pallas import tpu as pltpu
from jax.sharding import PartitionSpec as P

VMEM = pl.BlockSpec(memory_space=pltpu.VMEM)
ROWS_BY_COLUMNS = (((1,), (0,)), ((), ()))
ROWS_BY_ROWS = (((1,), (1,)), ((), ()))
RESIDENT_BYTES = 36 << 20
DEGREE_ROWS = 16


def call(body, out_shape, operands, scratch=(), limit=14 << 20, flops=0, name=None):
    return pl.pallas_call(
        body,
        out_shape=out_shape,
        in_specs=[VMEM] * len(operands),
        out_specs=jax.tree.map(lambda _: VMEM, out_shape),
        scratch_shapes=list(scratch),
        compiler_params=pltpu.CompilerParams(vmem_limit_bytes=limit),
        cost_estimate=pl.CostEstimate(flops=flops, bytes_accessed=0, transcendentals=0) if flops else None,
        name=name,
    )(*operands)


def f32(*shape):
    return jax.ShapeDtypeStruct(shape, jnp.float32)


def bf16(*shape):
    return jax.ShapeDtypeStruct(shape, jnp.bfloat16)


def halves(values):
    high = values.astype(jnp.bfloat16)
    return high, (values - high.astype(jnp.float32)).astype(jnp.bfloat16)


def thirds(values):
    high = values.astype(jnp.bfloat16).astype(jnp.float32)
    middle = (values - high).astype(jnp.bfloat16).astype(jnp.float32)
    return high, middle, values - high - middle


def pack(values):
    return jnp.concatenate([values[:, first : first + 128] for first in range(0, values.shape[1], 128)], axis=0)


def unpack(packed, lines, width):
    count = width // 128
    return jnp.concatenate([packed[block * lines : (block + 1) * lines] for block in range(count)], axis=1)


def pack_square(square):
    lines = square.shape[0] * square.shape[0] // 128
    return jnp.concatenate([square[first : first + lines] for first in range(0, square.shape[0], lines)], axis=1)


def unpack_square(packed, size):
    return jnp.concatenate([packed[:, first : first + size] for first in range(0, packed.shape[1], size)], axis=0)


def row_operand(points, left, span):
    width, features = points.shape
    high, low = halves(points)
    left[span, 0:features] = high
    left[span, features : 2 * features] = high
    left[span, 2 * features : 3 * features] = low
    first, second, third = thirds(0.5 * jnp.sum(points * points, axis=1, keepdims=True))
    lane = lax.broadcasted_iota(jnp.int32, (width, features), 1)
    tail = jnp.where(lane == 0, first, jnp.where(lane == 1, second, jnp.where(lane == 2, third, 0.0)))
    tail = jnp.where((lane > 2) & (lane < 6), -1.0, tail)
    left[span, 3 * features : 4 * features] = tail.astype(jnp.bfloat16)


def column_operand(points, right, span):
    features, width = points.shape
    high, low = halves(points)
    right[0:features, span] = high
    right[features : 2 * features, span] = low
    right[2 * features : 3 * features, span] = high
    first, second, third = thirds(0.5 * jnp.sum(points * points, axis=0, keepdims=True))
    line = lax.broadcasted_iota(jnp.int32, (features, width), 0)
    tail = jnp.where(line == 3, first, jnp.where(line == 4, second, jnp.where(line == 5, third, 0.0)))
    tail = jnp.where(line < 3, -1.0, tail)
    right[3 * features : 4 * features, span] = tail.astype(jnp.bfloat16)


def build_rows(left, right, high_ref, low_ref, totals, tile_rows=256, tile_columns=512):
    width = left.shape[0]
    for start in range(0, width, tile_rows):
        lines = slice(start, start + tile_rows)
        points = left[lines, :]
        total = jnp.zeros((tile_rows, 128), jnp.float32)
        for first in range(0, right.shape[1], tile_columns):
            span = slice(first, first + tile_columns)
            values = jnp.exp2(
                lax.dot_general(points, right[:, span], ROWS_BY_COLUMNS, preferred_element_type=jnp.float32)
            )
            high = values.astype(jnp.bfloat16)
            high_ref[lines, span] = high
            low_ref[lines, span] = (values - high.astype(jnp.float32)).astype(jnp.bfloat16)
            for lane in range(0, tile_columns, 128):
                total = total + values[:, lane : lane + 128]
        totals[lines, :] = total
    return jnp.sum(totals[...].T, axis=0, keepdims=True)


def point_scale(features):
    return math.sqrt(math.log2(math.e) / (0.25 * features))


def build_near_kernel(*refs, row_parts, column_parts):
    row_refs, column_refs = refs[:row_parts], (refs[0], *refs[row_parts : row_parts + column_parts - 1])
    outs = refs[row_parts + column_parts - 1 :]
    sums_ref, left_ref, right, totals = outs[2 * row_parts :]
    features, width = row_refs[0].shape
    scale = point_scale(features)
    for part, ref in enumerate(column_refs):
        column_operand(ref[...] * scale, right, slice(part * width, (part + 1) * width))
    sums_ref[...] = jnp.zeros_like(sums_ref)
    for part, (high_ref, low_ref) in enumerate(pairs(outs[: 2 * row_parts])):
        lines = slice(part * width, (part + 1) * width)
        row_operand(row_refs[part][...].T * scale, left_ref, lines)
        sums_ref[part : part + 1, :] = build_rows(left_ref.at[lines, :], right, high_ref, low_ref, totals)


def build_far_kernel(*refs, row_parts, column_parts):
    left_ref, near_right, near_sums_ref, start_ref, last_ref = refs[:5]
    column_refs, outs = refs[5 : 5 + column_parts], refs[5 + column_parts :]
    packed_ref, right, left, totals = outs[2 * row_parts + 4 :]
    vectors, width = start_ref.shape
    lanes = width // 128
    scale = point_scale(last_ref.shape[0])
    packed_ref[0 : vectors * lanes, :] = pack(start_ref[...])
    for part, ref in enumerate(column_refs):
        column_operand(ref[...] * scale, right, slice(part * width, (part + 1) * width))
    stores = pairs(outs[: 2 * row_parts + 4])

    def put(part, sums):
        line = (vectors + part) * lanes
        packed_ref[line : line + lanes, :] = pack(sums)

    for part in range(row_parts):
        lines = slice(part * width, (part + 1) * width)
        sums = build_rows(left_ref.at[lines, :], right, *stores[part], totals)
        put(part, near_sums_ref[part : part + 1, :] + sums)
    row_operand(last_ref[...].T * scale, left, slice(0, width))
    sums = build_rows(left, near_right, *stores[row_parts], totals)
    put(row_parts, sums + build_rows(left, right, *stores[row_parts + 1], totals))


def sweep(weights, parts, stores, block, initial=None, tile=256):
    rows = weights.shape[0] // 2
    width = stores[0][0].shape[0]
    pieces = []
    for first in range(0, width, tile):
        span = slice(block * width + first, block * width + first + tile)
        total = None if initial is None else initial[:, first : first + tile]
        for part, (high_ref, low_ref) in zip(parts, stores):
            lines = slice(part * width, (part + 1) * width)
            both = lax.dot_general(
                weights[:, lines], high_ref[:, span], ROWS_BY_COLUMNS, preferred_element_type=jnp.float32
            )
            last = lax.dot_general(
                weights[0:rows, lines], low_ref[:, span], ROWS_BY_COLUMNS, preferred_element_type=jnp.float32
            )
            term = both[0:rows] + both[rows:] + last
            total = term if total is None else total + term
        pieces.append(total)
    return jnp.concatenate(pieces, axis=1)


def pairs(refs):
    return list(zip(refs[0::2], refs[1::2]))


def place_of(block, odd):
    return block // 2, block % 2 + (2 if odd else 0)


def halved(refs, parts):
    return pairs(refs[: 2 * parts]), pairs(refs[2 * parts : 4 * parts])


def put_product(out_ref, product, vectors):
    width = product.shape[1]
    lanes = width // 128
    last = vectors * lanes
    out_ref[0:last, :] = pack(product[0:vectors])
    out_ref[last : last + 8, :] = jnp.zeros((8, 128), jnp.float32)
    out_ref[last : last + lanes, :] = pack(product[vectors : vectors + 1])


def first_kernel(*refs, parts):
    packed_refs, stores = refs[:parts], halved(refs[parts : 5 * parts], parts)
    out_ref, inverse_ref, weights = refs[5 * parts :]
    rows = weights.shape[0] // 2
    vectors = rows - DEGREE_ROWS
    width = inverse_ref.shape[1]
    lanes = width // 128

    def sums(peer, part):
        line = (vectors + part) * lanes
        return unpack(packed_refs[peer][line : line + lanes, :], 1, width)

    for part in range(parts):
        span = slice(part * width, (part + 1) * width)
        density = sums(0, part)
        for peer in range(1, parts):
            density = density + sums(peer, part ^ peer)
        inverse = 1.0 / density
        if part == 0:
            inverse_ref[...] = inverse
        line = lax.broadcasted_iota(jnp.int32, (DEGREE_ROWS, width), 0)
        for first, piece in (
            (0, unpack(packed_refs[part][0 : vectors * lanes, :], vectors, width) * inverse),
            (vectors, jnp.where(line == 0, inverse, 0.0)),
        ):
            high, low = halves(piece)
            last = first + piece.shape[0]
            weights[first:last, span] = high
            weights[rows + first : rows + last, span] = low
    for block in range(out_ref.shape[0]):
        half, place = place_of(block, True)
        put_product(out_ref.at[block], sweep(weights, range(parts), stores[half], place), vectors)


def far_kernel(*refs, parts, vectors):
    weights, stores, out_ref = refs[0], halved(refs[1 : 1 + 4 * parts], parts), refs[-1]
    for index in range(out_ref.shape[0]):
        half, place = place_of(1 + index, False)
        put_product(out_ref.at[index], sweep(weights, range(parts), stores[half], place), vectors)


def own_kernel(*refs, parts, vectors):
    weights, stores, out_ref = refs[0], pairs(refs[2 : 2 + 2 * parts]), refs[-1]
    put_product(out_ref, sweep(weights, range(parts), stores, 0), vectors)


def put_weights(weights, packed, place):
    vectors = weights.shape[0] // 2
    width = weights.shape[1] if place is None else packed.shape[0] // vectors * 128
    values = unpack(packed[0 : vectors * (width // 128), :], vectors, width)
    span = slice(0, width) if place is None else slice(place * width, (place + 1) * width)
    high, low = halves(values)
    weights[0:vectors, span] = high
    weights[vectors:, span] = low


def second_part_kernel(piece_ref, *refs):
    stores, (odd_ref, even_ref, weights) = pairs(refs[0:4]), refs[-3:]
    earlier = refs[4:-3] or (None, None)
    put_weights(weights, piece_ref[...], None)
    for odd, earlier_ref, out_ref in ((True, earlier[0], odd_ref), (False, earlier[1], even_ref)):
        for block in range(out_ref.shape[0]):
            half, place = place_of(block, odd)
            initial = None if earlier_ref is None else earlier_ref[block]
            out_ref[block] = sweep(weights, (0,), [stores[half]], place, initial)


def put_second(out_ref, product, gram):
    last = out_ref.shape[0] - gram.shape[0]
    out_ref[0:last, :] = pack(product)
    out_ref[last:, :] = gram


def second_odd_kernel(*refs, parts):
    piece_refs, refs = refs[:4], refs[4:]
    partial_ref, stores = refs[0], halved(refs[1 : 1 + 4 * parts], parts)
    out_ref, gram_ref, weights = refs[1 + 4 * parts :]
    last = piece_refs[0].shape[0] - gram_ref.shape[0]
    gram = piece_refs[0][last:, :]
    for ref in piece_refs[1:]:
        gram = gram + ref[last:, :]
    gram_ref[...] = gram
    for part, ref in enumerate(piece_refs[-parts:]):
        put_weights(weights, ref[...], part)
    for block in range(out_ref.shape[0]):
        half, place = place_of(block, True)
        product = sweep(weights, range(parts), stores[half], place, partial_ref[block])
        put_second(out_ref.at[block], product, gram)


def second_even_kernel(*refs, parts):
    weights, gram_ref, partial_ref = refs[:3]
    stores, out_ref = halved(refs[3 : 3 + 4 * parts], parts), refs[-1]
    for index in range(out_ref.shape[0]):
        half, place = place_of(1 + index, False)
        product = sweep(weights, range(parts), stores[half], place, partial_ref[1 + index])
        put_second(out_ref.at[index], product, gram_ref[...])


def second_own_kernel(*refs, parts):
    weights, gram_ref, partial_ref = refs[:3]
    stores, out_ref = pairs(refs[4 : 4 + 2 * parts]), refs[-1]
    put_second(out_ref, sweep(weights, range(parts), stores, 0, partial_ref[0]), gram_ref[...])


def exact(left, right, dims):
    return lax.dot_general(
        left, right, dims, precision=lax.Precision.HIGHEST, preferred_element_type=jnp.float32
    )


def add_up(refs):
    total = refs[0][...]
    for ref in refs[1:]:
        total = total + ref[...]
    return total


def grown_kernel(*refs):
    inverse_ref, piece_refs, (grown_ref, degree_ref) = refs[0], refs[1:-2], refs[-2:]
    width = degree_ref.shape[1]
    lanes = width // 128
    vectors = (grown_ref.shape[0] - 8) // lanes
    total = add_up(piece_refs)
    last = vectors * lanes
    degree = unpack(total[last : last + lanes], 1, width)
    grown = unpack(total[0:last], vectors, width) / degree
    degree_ref[...] = degree
    grown_ref[0:last, :] = pack(grown * inverse_ref[...])
    grown_ref[last:, :] = pack_square(exact(grown, grown, ROWS_BY_ROWS))


def inverse_factor(gram, panel=16):
    size = gram.shape[0]
    shape = (size, 2 * size)
    line = lax.broadcasted_iota(jnp.int32, (size, size), 0)
    lane = lax.broadcasted_iota(jnp.int32, (size, size), 1)
    table = jnp.concatenate([gram, jnp.where(line == lane, 1.0, 0.0)], axis=1)
    tall = lax.broadcasted_iota(jnp.int32, shape, 0)
    pivots = jnp.zeros(shape, jnp.float32)
    for first in range(0, size, panel):
        columns = [jnp.broadcast_to(table[:, step : step + 1], shape) for step in range(first, first + panel)]
        for place, step in enumerate(range(first, first + panel)):
            pivot = columns[place][step : step + 1, :]
            pivots = jnp.where(tall == step, pivot, pivots)
            factor = jnp.where(tall > step, columns[place] * (1.0 / pivot), 0.0)
            for later in range(place + 1, panel):
                columns[later] = columns[later] - factor * columns[later][step : step + 1, :]
            table = table - factor * table[step : step + 1, :]
    return table[:, size:] * lax.rsqrt(pivots[:, size:])


def grown_two_kernel(*refs, count):
    degree_ref, piece_refs, (grown_ref, gram_ref) = refs[0], refs[1:-2], refs[-2:]
    vectors, width = grown_ref.shape
    total = add_up(piece_refs)
    last = vectors * (width // 128)
    factor = inverse_factor(unpack_square(total[last:], vectors) * (1.0 / count))
    product = unpack(total[0:last], vectors, width)
    grown = exact(factor, product / degree_ref[...], ROWS_BY_COLUMNS)
    grown_ref[...] = grown
    gram_ref[...] = pack_square(exact(grown, grown, ROWS_BY_ROWS))


def finish_kernel(*refs, count):
    grown_ref, gram_refs, out_ref = refs[0], refs[1:-1], refs[-1]
    gram = unpack_square(add_up(gram_refs), grown_ref.shape[0])
    out_ref[...] = exact(inverse_factor(gram * (1.0 / count)), grown_ref[...], ROWS_BY_COLUMNS)


def swap(values, mask):
    size = lax.axis_size(("row", "col"))
    return lax.ppermute(values, ("row", "col"), [(index, index ^ mask) for index in range(size)])


def fetch_kernel(frames_ref, start_ref, own_ref, own_start_ref, sems):
    copies = [
        pltpu.make_async_copy(source, target, sems.at[index])
        for index, (source, target) in enumerate(((frames_ref, own_ref), (start_ref, own_start_ref)))
    ]
    for copy in copies:
        copy.start()
    for copy in copies:
        copy.wait()


def fetch(frames, start):
    return pl.pallas_call(
        fetch_kernel,
        out_shape=(f32(*frames.shape), f32(*start.shape)),
        in_specs=[pl.BlockSpec(memory_space=pltpu.HBM)] * 2,
        out_specs=(VMEM, VMEM),
        scratch_shapes=[pltpu.SemaphoreType.DMA((2,))],
        compiler_params=pltpu.CompilerParams(vmem_limit_bytes=1 << 20),
        cost_estimate=pl.CostEstimate(flops=1 << 34, bytes_accessed=0, transcendentals=0),
        name="fetch",
    )(pltpu.with_memory_space_constraint(frames, pltpu.HBM), pltpu.with_memory_space_constraint(start, pltpu.HBM))


def resident_shards(frames, start):
    row_size, column_size = lax.axis_size("row"), lax.axis_size("col")
    count = frames.shape[1] * row_size * column_size
    features, width = frames.shape
    vectors = start.shape[0]

    core, across, skip = column_size, column_size * row_size // 2, column_size // 2
    beside, along = 2 * core, 1
    near = (across, skip, across | skip)
    far = (beside, along, beside | along)
    parts, half = 4, 4

    skip_piece = swap(frames, skip)
    own, own_start = fetch(frames, start)
    beside_piece = swap(own, beside)
    along_piece = swap(own, along)
    across_piece = swap(swap(own, across | core), core)
    corner_piece = swap(along_piece, beside)
    row_pieces = [across_piece, skip_piece]
    last_piece = swap(skip_piece, across)
    near_columns = [beside_piece, swap(own, core), swap(beside_piece, core)]
    far_columns = [along_piece, corner_piece, swap(along_piece, core), swap(corner_piece, core)]

    operands = 4 * features
    columns = half * width
    lanes = width // 128
    packed_lines = vectors * lanes + 8
    rest = parts - 1
    stored = (bf16(width, columns),) * 2
    totals = pltpu.VMEM((width, 128), jnp.float32)
    *near_store, sums, left, right = call(
        functools.partial(build_near_kernel, row_parts=rest, column_parts=half),
        (*(stored * rest), f32(8, width), bf16(rest * width, operands), bf16(operands, columns)),
        (own, *row_pieces, *near_columns),
        scratch=(totals,),
        flops=1,
        name="build_near",
    )
    *far_store, last_high, last_low, far_high, far_low, packed = call(
        functools.partial(build_far_kernel, row_parts=rest, column_parts=half),
        (*(stored * (rest + 2)), f32((vectors + parts) * lanes, 128)),
        (left, right, sums, own_start, last_piece, *far_columns),
        scratch=(
            pltpu.VMEM((operands, columns), jnp.bfloat16),
            pltpu.VMEM((width, operands), jnp.bfloat16),
            totals,
        ),
        flops=1,
        name="build_far",
    )
    near_store = (*near_store, last_high, last_low)
    far_store = (*far_store, far_high, far_low)
    all_packed = [packed] + [swap(packed, mask) for mask in near]

    def spread(odds, evens):
        odds = swap(odds, core)
        both = evens + odds[1:]
        return odds[0], both, [swap(both[place], mask) for place, mask in enumerate(far)]

    def total_gram(gram):
        gram = gram + swap(gram, core)
        gram = functools.reduce(jnp.add, [swap(gram, mask | core) for mask in far], gram)
        return [gram] + [swap(gram, mask | core) for mask in near]

    rows = vectors + DEGREE_ROWS
    block = 2 * 3 * rows * parts * width * width
    odds, inverse, weights = call(
        functools.partial(first_kernel, parts=parts),
        (f32(half, packed_lines, 128), f32(1, width), bf16(2 * rows, parts * width)),
        (*all_packed, *near_store, *far_store),
        flops=half * block,
        name="first_odd",
    )
    evens = call(
        functools.partial(far_kernel, parts=parts, vectors=vectors),
        f32(half - 1, packed_lines, 128),
        (weights, *near_store, *far_store),
        flops=(half - 1) * block,
        name="first_even",
    )
    own_odd, both, others = spread(odds, evens)
    own_even = call(
        functools.partial(own_kernel, parts=parts, vectors=vectors),
        f32(packed_lines, 128),
        (weights, both, *near_store),
        flops=block,
        name="first_own",
    )
    weighted, degree = call(
        grown_kernel,
        (f32(packed_lines, 128), f32(1, width)),
        (inverse, own_even, own_odd, *others),
        name="grown",
    )
    pieces = [weighted] + [swap(weighted, mask) for mask in near]
    partial = ()
    for part in range(2):
        partial = call(
            second_part_kernel,
            (f32(half, vectors, width),) * 2,
            (pieces[part], *near_store[2 * part : 2 * part + 2], *far_store[2 * part : 2 * part + 2], *partial),
            scratch=(pltpu.VMEM((2 * vectors, width), jnp.bfloat16),),
            flops=2 * half * block // parts,
            name="second_part",
        )
    odd_partial, even_partial = partial
    rest = parts - 2
    near_store, far_store = near_store[4:], far_store[4:]
    odds, gram, weights = call(
        functools.partial(second_odd_kernel, parts=rest),
        (f32(half, packed_lines, 128), f32(8, 128), bf16(2 * vectors, rest * width)),
        (*pieces, odd_partial, *near_store, *far_store),
        flops=half * block,
        name="second_odd",
    )
    evens = call(
        functools.partial(second_even_kernel, parts=rest),
        f32(half - 1, packed_lines, 128),
        (weights, gram, even_partial, *near_store, *far_store),
        flops=(half - 1) * block,
        name="second_even",
    )
    own_odd, both, others = spread(odds, evens)
    own_even = call(
        functools.partial(second_own_kernel, parts=rest),
        f32(packed_lines, 128),
        (weights, gram, even_partial, both, *near_store),
        flops=block,
        name="second_own",
    )
    grown_two, gram_two = call(
        functools.partial(grown_two_kernel, count=count),
        (f32(vectors, width), f32(8, 128)),
        (degree, own_even, own_odd, *others),
        name="grown_two",
    )
    return call(
        functools.partial(finish_kernel, count=count),
        f32(vectors, width),
        (grown_two, *total_gram(gram_two)),
        name="finish",
    )


def build_block(block_points, block_squares, column_points, column_squares):
    products = lax.dot_general(
        block_points, column_points, (((0,), (0,)), ((), ())), precision=lax.Precision.HIGHEST
    )
    distance = block_squares[:, None] + column_squares[None, :] - 2.0 * products
    return jnp.exp(-distance / (0.5 * block_points.shape[0]))


def stored_shards(frames, start):
    block_points = lax.all_gather(frames, "col", axis=1, tiled=True)
    column_points = lax.all_gather(frames, "row", axis=1, tiled=True)
    block_squares = jnp.sum(block_points * block_points, axis=0)
    column_squares = jnp.sum(column_points * column_points, axis=0)
    frame_count = frames.shape[1] * lax.axis_size("row") * lax.axis_size("col")
    block_rows = block_points.shape[1]
    height = min(512, block_rows)
    stored = [
        build_block(
            block_points[:, first : first + height],
            block_squares[first : first + height],
            column_points,
            column_squares,
        )
        for first in range(0, block_rows, height)
    ]

    def settle(partial_value):
        return lax.psum_scatter(partial_value, "col", scatter_dimension=1, tiled=True)

    def kernel_product(weights):
        spread_weights = lax.all_gather(weights, "row", axis=1, tiled=True)
        return settle(
            jnp.concatenate([exact(spread_weights, part, ROWS_BY_ROWS) for part in stored], axis=1)
        )

    def orthonormal(vectors):
        gram = lax.psum(exact(vectors, vectors, ROWS_BY_ROWS), ("row", "col")) / frame_count
        return jax.scipy.linalg.solve_triangular(jnp.linalg.cholesky(gram), vectors, lower=True)

    sums = jnp.concatenate([jnp.sum(part, axis=1)[None, :] for part in stored], axis=1)
    inverse = 1.0 / settle(sums)
    degree = kernel_product(inverse)
    basis_one = orthonormal(kernel_product(start * inverse) / degree)
    return orthonormal(kernel_product(basis_one * inverse) / degree)


def shards(frames, start):
    row_size, column_size = lax.axis_size("row"), lax.axis_size("col")
    entries = row_size * column_size * frames.shape[1] ** 2
    shapes = (row_size, column_size, start.shape[0], frames.shape[1] % 128)
    if shapes == (8, 4, 32, 0) and 4 * entries <= RESIDENT_BYTES:
        return resident_shards(frames, start)
    return stored_shards(frames, start)


def solution(mesh):
    return jax.shard_map(
        shards,
        mesh=mesh,
        in_specs=(P(None, ("row", "col")), P(None, ("row", "col"))),
        out_specs=P(None, ("row", "col")),
        check_vma=False,
    )
```

```python
import functools
import math
import jax
import jax.numpy as jnp
from jax import lax
from jax.experimental import pallas as pl
from jax.experimental.pallas import tpu as pltpu
from jax.sharding import PartitionSpec as P

VMEM = pl.BlockSpec(memory_space=pltpu.VMEM)
ROWS_BY_COLUMNS = (((1,), (0,)), ((), ()))
ROWS_BY_ROWS = (((1,), (1,)), ((), ()))
RESIDENT_BYTES = 36 << 20
DEGREE_ROWS = 16


def call(body, out_shape, operands, scratch=(), limit=14 << 20, flops=0, name=None):
    return pl.pallas_call(
        body,
        out_shape=out_shape,
        in_specs=[VMEM] * len(operands),
        out_specs=jax.tree.map(lambda _: VMEM, out_shape),
        scratch_shapes=list(scratch),
        compiler_params=pltpu.CompilerParams(vmem_limit_bytes=limit),
        cost_estimate=pl.CostEstimate(flops=flops, bytes_accessed=0, transcendentals=0) if flops else None,
        name=name,
    )(*operands)


def f32(*shape):
    return jax.ShapeDtypeStruct(shape, jnp.float32)


def bf16(*shape):
    return jax.ShapeDtypeStruct(shape, jnp.bfloat16)


def halves(values):
    high = values.astype(jnp.bfloat16)
    return high, (values - high.astype(jnp.float32)).astype(jnp.bfloat16)


def thirds(values):
    high = values.astype(jnp.bfloat16).astype(jnp.float32)
    middle = (values - high).astype(jnp.bfloat16).astype(jnp.float32)
    return high, middle, values - high - middle


def pack(values):
    return jnp.concatenate([values[:, first : first + 128] for first in range(0, values.shape[1], 128)], axis=0)


def unpack(packed, lines, width):
    count = width // 128
    return jnp.concatenate([packed[block * lines : (block + 1) * lines] for block in range(count)], axis=1)


def pack_square(square):
    lines = square.shape[0] * square.shape[0] // 128
    return jnp.concatenate([square[first : first + lines] for first in range(0, square.shape[0], lines)], axis=1)


def unpack_square(packed, size):
    return jnp.concatenate([packed[:, first : first + size] for first in range(0, packed.shape[1], size)], axis=0)


def row_operand(points, left, span):
    width, features = points.shape
    high, low = halves(points)
    left[span, 0:features] = high
    left[span, features : 2 * features] = high
    left[span, 2 * features : 3 * features] = low
    first, second, third = thirds(0.5 * jnp.sum(points * points, axis=1, keepdims=True))
    lane = lax.broadcasted_iota(jnp.int32, (width, features), 1)
    tail = jnp.where(lane == 0, first, jnp.where(lane == 1, second, jnp.where(lane == 2, third, 0.0)))
    tail = jnp.where((lane > 2) & (lane < 6), -1.0, tail)
    left[span, 3 * features : 4 * features] = tail.astype(jnp.bfloat16)


def column_operand(points, right, span):
    features, width = points.shape
    high, low = halves(points)
    right[0:features, span] = high
    right[features : 2 * features, span] = low
    right[2 * features : 3 * features, span] = high
    first, second, third = thirds(0.5 * jnp.sum(points * points, axis=0, keepdims=True))
    line = lax.broadcasted_iota(jnp.int32, (features, width), 0)
    tail = jnp.where(line == 3, first, jnp.where(line == 4, second, jnp.where(line == 5, third, 0.0)))
    tail = jnp.where(line < 3, -1.0, tail)
    right[3 * features : 4 * features, span] = tail.astype(jnp.bfloat16)


def build_rows(left, right, high_ref, low_ref, totals, tile_rows=256, tile_columns=512):
    width = left.shape[0]
    for start in range(0, width, tile_rows):
        lines = slice(start, start + tile_rows)
        points = left[lines, :]
        total = jnp.zeros((tile_rows, 128), jnp.float32)
        for first in range(0, right.shape[1], tile_columns):
            span = slice(first, first + tile_columns)
            values = jnp.exp2(
                lax.dot_general(points, right[:, span], ROWS_BY_COLUMNS, preferred_element_type=jnp.float32)
            )
            high = values.astype(jnp.bfloat16)
            high_ref[lines, span] = high
            low_ref[lines, span] = (values - high.astype(jnp.float32)).astype(jnp.bfloat16)
            for lane in range(0, tile_columns, 128):
                total = total + values[:, lane : lane + 128]
        totals[lines, :] = total
    return jnp.sum(totals[...].T, axis=0, keepdims=True)


def point_scale(features):
    return math.sqrt(math.log2(math.e) / (0.25 * features))


def build_near_kernel(*refs, row_parts, column_parts):
    row_refs, column_refs = refs[:row_parts], (refs[0], *refs[row_parts : row_parts + column_parts - 1])
    outs = refs[row_parts + column_parts - 1 :]
    sums_ref, left_ref, right, totals = outs[2 * row_parts :]
    features, width = row_refs[0].shape
    scale = point_scale(features)
    for part, ref in enumerate(column_refs):
        column_operand(ref[...] * scale, right, slice(part * width, (part + 1) * width))
    sums_ref[...] = jnp.zeros_like(sums_ref)
    for part, (high_ref, low_ref) in enumerate(pairs(outs[: 2 * row_parts])):
        lines = slice(part * width, (part + 1) * width)
        row_operand(row_refs[part][...].T * scale, left_ref, lines)
        sums_ref[part : part + 1, :] = build_rows(left_ref.at[lines, :], right, high_ref, low_ref, totals)


def build_far_kernel(*refs, row_parts, column_parts):
    left_ref, near_right, near_sums_ref, start_ref, last_ref = refs[:5]
    column_refs, outs = refs[5 : 5 + column_parts], refs[5 + column_parts :]
    packed_ref, right, left, totals = outs[2 * row_parts + 4 :]
    vectors, width = start_ref.shape
    lanes = width // 128
    scale = point_scale(last_ref.shape[0])
    packed_ref[0 : vectors * lanes, :] = pack(start_ref[...])
    for part, ref in enumerate(column_refs):
        column_operand(ref[...] * scale, right, slice(part * width, (part + 1) * width))
    stores = pairs(outs[: 2 * row_parts + 4])

    def put(part, sums):
        line = (vectors + part) * lanes
        packed_ref[line : line + lanes, :] = pack(sums)

    for part in range(row_parts):
        lines = slice(part * width, (part + 1) * width)
        sums = build_rows(left_ref.at[lines, :], right, *stores[part], totals)
        put(part, near_sums_ref[part : part + 1, :] + sums)
    row_operand(last_ref[...].T * scale, left, slice(0, width))
    sums = build_rows(left, near_right, *stores[row_parts], totals)
    put(row_parts, sums + build_rows(left, right, *stores[row_parts + 1], totals))


def sweep(weights, parts, stores, block, initial=None, tile=256):
    rows = weights.shape[0] // 2
    width = stores[0][0].shape[0]
    pieces = []
    for first in range(0, width, tile):
        span = slice(block * width + first, block * width + first + tile)
        total = None if initial is None else initial[:, first : first + tile]
        for part, (high_ref, low_ref) in zip(parts, stores):
            lines = slice(part * width, (part + 1) * width)
            both = lax.dot_general(
                weights[:, lines], high_ref[:, span], ROWS_BY_COLUMNS, preferred_element_type=jnp.float32
            )
            last = lax.dot_general(
                weights[0:rows, lines], low_ref[:, span], ROWS_BY_COLUMNS, preferred_element_type=jnp.float32
            )
            term = both[0:rows] + both[rows:] + last
            total = term if total is None else total + term
        pieces.append(total)
    return jnp.concatenate(pieces, axis=1)


def pairs(refs):
    return list(zip(refs[0::2], refs[1::2]))


def place_of(block, odd):
    return block // 2, block % 2 + (2 if odd else 0)


def halved(refs, parts):
    return pairs(refs[: 2 * parts]), pairs(refs[2 * parts : 4 * parts])


def put_product(out_ref, product, vectors):
    width = product.shape[1]
    lanes = width // 128
    last = vectors * lanes
    out_ref[0:last, :] = pack(product[0:vectors])
    out_ref[last : last + 8, :] = jnp.zeros((8, 128), jnp.float32)
    out_ref[last : last + lanes, :] = pack(product[vectors : vectors + 1])


def first_kernel(*refs, parts):
    packed_refs, stores = refs[:parts], halved(refs[parts : 5 * parts], parts)
    out_ref, inverse_ref, weights = refs[5 * parts :]
    rows = weights.shape[0] // 2
    vectors = rows - DEGREE_ROWS
    width = inverse_ref.shape[1]
    lanes = width // 128

    def sums(peer, part):
        line = (vectors + part) * lanes
        return unpack(packed_refs[peer][line : line + lanes, :], 1, width)

    for part in range(parts):
        span = slice(part * width, (part + 1) * width)
        density = sums(0, part)
        for peer in range(1, parts):
            density = density + sums(peer, part ^ peer)
        inverse = 1.0 / density
        if part == 0:
            inverse_ref[...] = inverse
        line = lax.broadcasted_iota(jnp.int32, (DEGREE_ROWS, width), 0)
        for first, piece in (
            (0, unpack(packed_refs[part][0 : vectors * lanes, :], vectors, width) * inverse),
            (vectors, jnp.where(line == 0, inverse, 0.0)),
        ):
            high, low = halves(piece)
            last = first + piece.shape[0]
            weights[first:last, span] = high
            weights[rows + first : rows + last, span] = low
    for block in range(out_ref.shape[0]):
        half, place = place_of(block, True)
        put_product(out_ref.at[block], sweep(weights, range(parts), stores[half], place), vectors)


def far_kernel(*refs, parts, vectors):
    weights, stores, out_ref = refs[0], halved(refs[1 : 1 + 4 * parts], parts), refs[-1]
    for index in range(out_ref.shape[0]):
        half, place = place_of(1 + index, False)
        put_product(out_ref.at[index], sweep(weights, range(parts), stores[half], place), vectors)


def own_kernel(*refs, parts, vectors):
    weights, stores, out_ref = refs[0], pairs(refs[2 : 2 + 2 * parts]), refs[-1]
    put_product(out_ref, sweep(weights, range(parts), stores, 0), vectors)


def put_weights(weights, packed, place):
    vectors = weights.shape[0] // 2
    width = weights.shape[1] if place is None else packed.shape[0] // vectors * 128
    values = unpack(packed[0 : vectors * (width // 128), :], vectors, width)
    span = slice(0, width) if place is None else slice(place * width, (place + 1) * width)
    high, low = halves(values)
    weights[0:vectors, span] = high
    weights[vectors:, span] = low


def second_part_kernel(piece_ref, *refs):
    stores, (odd_ref, even_ref, weights) = pairs(refs[0:4]), refs[-3:]
    earlier = refs[4:-3] or (None, None)
    put_weights(weights, piece_ref[...], None)
    for odd, earlier_ref, out_ref in ((True, earlier[0], odd_ref), (False, earlier[1], even_ref)):
        for block in range(out_ref.shape[0]):
            half, place = place_of(block, odd)
            initial = None if earlier_ref is None else earlier_ref[block]
            out_ref[block] = sweep(weights, (0,), [stores[half]], place, initial)


def put_second(out_ref, product, gram):
    last = out_ref.shape[0] - gram.shape[0]
    out_ref[0:last, :] = pack(product)
    out_ref[last:, :] = gram


def second_odd_kernel(*refs, parts):
    piece_refs, refs = refs[:4], refs[4:]
    partial_ref, stores = refs[0], halved(refs[1 : 1 + 4 * parts], parts)
    out_ref, gram_ref, weights = refs[1 + 4 * parts :]
    last = piece_refs[0].shape[0] - gram_ref.shape[0]
    gram = piece_refs[0][last:, :]
    for ref in piece_refs[1:]:
        gram = gram + ref[last:, :]
    gram_ref[...] = gram
    for part, ref in enumerate(piece_refs[-parts:]):
        put_weights(weights, ref[...], part)
    for block in range(out_ref.shape[0]):
        half, place = place_of(block, True)
        product = sweep(weights, range(parts), stores[half], place, partial_ref[block])
        put_second(out_ref.at[block], product, gram)


def second_even_kernel(*refs, parts):
    weights, gram_ref, partial_ref = refs[:3]
    stores, out_ref = halved(refs[3 : 3 + 4 * parts], parts), refs[-1]
    for index in range(out_ref.shape[0]):
        half, place = place_of(1 + index, False)
        product = sweep(weights, range(parts), stores[half], place, partial_ref[1 + index])
        put_second(out_ref.at[index], product, gram_ref[...])


def second_own_kernel(*refs, parts):
    weights, gram_ref, partial_ref = refs[:3]
    stores, out_ref = pairs(refs[4 : 4 + 2 * parts]), refs[-1]
    put_second(out_ref, sweep(weights, range(parts), stores, 0, partial_ref[0]), gram_ref[...])


def exact(left, right, dims):
    return lax.dot_general(
        left, right, dims, precision=lax.Precision.HIGHEST, preferred_element_type=jnp.float32
    )


def add_up(refs):
    total = refs[0][...]
    for ref in refs[1:]:
        total = total + ref[...]
    return total


def grown_kernel(*refs):
    inverse_ref, piece_refs, (grown_ref, degree_ref) = refs[0], refs[1:-2], refs[-2:]
    width = degree_ref.shape[1]
    lanes = width // 128
    vectors = (grown_ref.shape[0] - 8) // lanes
    total = add_up(piece_refs)
    last = vectors * lanes
    degree = unpack(total[last : last + lanes], 1, width)
    grown = unpack(total[0:last], vectors, width) / degree
    degree_ref[...] = degree
    grown_ref[0:last, :] = pack(grown * inverse_ref[...])
    grown_ref[last:, :] = pack_square(exact(grown, grown, ROWS_BY_ROWS))


def inverse_factor(gram, panel=16):
    size = gram.shape[0]
    shape = (size, 2 * size)
    line = lax.broadcasted_iota(jnp.int32, (size, size), 0)
    lane = lax.broadcasted_iota(jnp.int32, (size, size), 1)
    table = jnp.concatenate([gram, jnp.where(line == lane, 1.0, 0.0)], axis=1)
    tall = lax.broadcasted_iota(jnp.int32, shape, 0)
    pivots = jnp.zeros(shape, jnp.float32)
    for first in range(0, size, panel):
        columns = [jnp.broadcast_to(table[:, step : step + 1], shape) for step in range(first, first + panel)]
        for place, step in enumerate(range(first, first + panel)):
            pivot = columns[place][step : step + 1, :]
            pivots = jnp.where(tall == step, pivot, pivots)
            factor = jnp.where(tall > step, columns[place] * (1.0 / pivot), 0.0)
            for later in range(place + 1, panel):
                columns[later] = columns[later] - factor * columns[later][step : step + 1, :]
            table = table - factor * table[step : step + 1, :]
    return table[:, size:] * lax.rsqrt(pivots[:, size:])


def grown_two_kernel(*refs, count):
    degree_ref, piece_refs, (grown_ref, gram_ref) = refs[0], refs[1:-2], refs[-2:]
    vectors, width = grown_ref.shape
    total = add_up(piece_refs)
    last = vectors * (width // 128)
    factor = inverse_factor(unpack_square(total[last:], vectors) * (1.0 / count))
    product = unpack(total[0:last], vectors, width)
    grown = exact(factor, product / degree_ref[...], ROWS_BY_COLUMNS)
    grown_ref[...] = grown
    gram_ref[...] = pack_square(exact(grown, grown, ROWS_BY_ROWS))


def finish_kernel(*refs, count):
    grown_ref, gram_refs, out_ref = refs[0], refs[1:-1], refs[-1]
    gram = unpack_square(add_up(gram_refs), grown_ref.shape[0])
    out_ref[...] = exact(inverse_factor(gram * (1.0 / count)), grown_ref[...], ROWS_BY_COLUMNS)


def swap(values, mask):
    size = lax.axis_size(("row", "col"))
    return lax.ppermute(values, ("row", "col"), [(index, index ^ mask) for index in range(size)])


def fetch_kernel(frames_ref, start_ref, own_ref, own_start_ref, sems):
    copies = [
        pltpu.make_async_copy(source, target, sems.at[index])
        for index, (source, target) in enumerate(((frames_ref, own_ref), (start_ref, own_start_ref)))
    ]
    for copy in copies:
        copy.start()
    for copy in copies:
        copy.wait()


def fetch(frames, start):
    return pl.pallas_call(
        fetch_kernel,
        out_shape=(f32(*frames.shape), f32(*start.shape)),
        in_specs=[pl.BlockSpec(memory_space=pltpu.HBM)] * 2,
        out_specs=(VMEM, VMEM),
        scratch_shapes=[pltpu.SemaphoreType.DMA((2,))],
        compiler_params=pltpu.CompilerParams(vmem_limit_bytes=1 << 20),
        cost_estimate=pl.CostEstimate(flops=1 << 34, bytes_accessed=0, transcendentals=0),
        name="fetch",
    )(pltpu.with_memory_space_constraint(frames, pltpu.HBM), pltpu.with_memory_space_constraint(start, pltpu.HBM))


def resident_shards(frames, start):
    row_size, column_size = lax.axis_size("row"), lax.axis_size("col")
    count = frames.shape[1] * row_size * column_size
    features, width = frames.shape
    vectors = start.shape[0]

    core, across, skip = column_size, column_size * row_size // 2, column_size // 2
    beside, along = 2 * core, 1
    near = (across, skip, across | skip)
    far = (beside, along, beside | along)
    parts, half = 4, 4

    skip_piece = swap(frames, skip)
    own, own_start = fetch(frames, start)
    beside_piece = swap(own, beside)
    along_piece = swap(own, along)
    across_piece = swap(swap(own, across | core), core)
    corner_piece = swap(along_piece, beside)
    row_pieces = [across_piece, skip_piece]
    last_piece = swap(skip_piece, across)
    near_columns = [beside_piece, swap(own, core), swap(beside_piece, core)]
    far_columns = [along_piece, corner_piece, swap(along_piece, core), swap(corner_piece, core)]

    operands = 4 * features
    columns = half * width
    lanes = width // 128
    packed_lines = vectors * lanes + 8
    rest = parts - 1
    stored = (bf16(width, columns),) * 2
    totals = pltpu.VMEM((width, 128), jnp.float32)
    *near_store, sums, left, right = call(
        functools.partial(build_near_kernel, row_parts=rest, column_parts=half),
        (*(stored * rest), f32(8, width), bf16(rest * width, operands), bf16(operands, columns)),
        (own, *row_pieces, *near_columns),
        scratch=(totals,),
        flops=1,
        name="build_near",
    )
    *far_store, last_high, last_low, far_high, far_low, packed = call(
        functools.partial(build_far_kernel, row_parts=rest, column_parts=half),
        (*(stored * (rest + 2)), f32((vectors + parts) * lanes, 128)),
        (left, right, sums, own_start, last_piece, *far_columns),
        scratch=(
            pltpu.VMEM((operands, columns), jnp.bfloat16),
            pltpu.VMEM((width, operands), jnp.bfloat16),
            totals,
        ),
        flops=1,
        name="build_far",
    )
    near_store = (*near_store, last_high, last_low)
    far_store = (*far_store, far_high, far_low)
    all_packed = [packed] + [swap(packed, mask) for mask in near]

    def spread(odds, evens):
        odds = swap(odds, core)
        both = evens + odds[1:]
        return odds[0], both, [swap(both[place], mask) for place, mask in enumerate(far)]

    def total_gram(gram):
        gram = gram + swap(gram, core)
        gram = functools.reduce(jnp.add, [swap(gram, mask | core) for mask in near], gram)
        return [gram] + [swap(gram, mask | core) for mask in far]

    rows = vectors + DEGREE_ROWS
    block = 2 * 3 * rows * parts * width * width
    odds, inverse, weights = call(
        functools.partial(first_kernel, parts=parts),
        (f32(half, packed_lines, 128), f32(1, width), bf16(2 * rows, parts * width)),
        (*all_packed, *near_store, *far_store),
        flops=half * block,
        name="first_odd",
    )
    evens = call(
        functools.partial(far_kernel, parts=parts, vectors=vectors),
        f32(half - 1, packed_lines, 128),
        (weights, *near_store, *far_store),
        flops=(half - 1) * block,
        name="first_even",
    )
    own_odd, both, others = spread(odds, evens)
    own_even = call(
        functools.partial(own_kernel, parts=parts, vectors=vectors),
        f32(packed_lines, 128),
        (weights, both, *near_store),
        flops=block,
        name="first_own",
    )
    weighted, degree = call(
        grown_kernel,
        (f32(packed_lines, 128), f32(1, width)),
        (inverse, own_even, own_odd, *others),
        name="grown",
    )
    pieces = [weighted] + [swap(weighted, mask) for mask in near]
    partial = ()
    for part in range(2):
        partial = call(
            second_part_kernel,
            (f32(half, vectors, width),) * 2,
            (pieces[part], *near_store[2 * part : 2 * part + 2], *far_store[2 * part : 2 * part + 2], *partial),
            scratch=(pltpu.VMEM((2 * vectors, width), jnp.bfloat16),),
            flops=2 * half * block // parts,
            name="second_part",
        )
    odd_partial, even_partial = partial
    rest = parts - 2
    near_store, far_store = near_store[4:], far_store[4:]
    odds, gram, weights = call(
        functools.partial(second_odd_kernel, parts=rest),
        (f32(half, packed_lines, 128), f32(8, 128), bf16(2 * vectors, rest * width)),
        (*pieces, odd_partial, *near_store, *far_store),
        flops=half * block,
        name="second_odd",
    )
    evens = call(
        functools.partial(second_even_kernel, parts=rest),
        f32(half - 1, packed_lines, 128),
        (weights, gram, even_partial, *near_store, *far_store),
        flops=(half - 1) * block,
        name="second_even",
    )
    own_odd, both, others = spread(odds, evens)
    own_even = call(
        functools.partial(second_own_kernel, parts=rest),
        f32(packed_lines, 128),
        (weights, gram, even_partial, both, *near_store),
        flops=block,
        name="second_own",
    )
    grown_two, gram_two = call(
        functools.partial(grown_two_kernel, count=count),
        (f32(vectors, width), f32(8, 128)),
        (degree, own_even, own_odd, *others),
        name="grown_two",
    )
    return call(
        functools.partial(finish_kernel, count=count),
        f32(vectors, width),
        (grown_two, *total_gram(gram_two)),
        name="finish",
    )


def build_block(block_points, block_squares, column_points, column_squares):
    products = lax.dot_general(
        block_points, column_points, (((0,), (0,)), ((), ())), precision=lax.Precision.HIGHEST
    )
    distance = block_squares[:, None] + column_squares[None, :] - 2.0 * products
    return jnp.exp(-distance / (0.5 * block_points.shape[0]))


def stored_shards(frames, start):
    block_points = lax.all_gather(frames, "col", axis=1, tiled=True)
    column_points = lax.all_gather(frames, "row", axis=1, tiled=True)
    block_squares = jnp.sum(block_points * block_points, axis=0)
    column_squares = jnp.sum(column_points * column_points, axis=0)
    frame_count = frames.shape[1] * lax.axis_size("row") * lax.axis_size("col")
    block_rows = block_points.shape[1]
    height = min(512, block_rows)
    stored = [
        build_block(
            block_points[:, first : first + height],
            block_squares[first : first + height],
            column_points,
            column_squares,
        )
        for first in range(0, block_rows, height)
    ]

    def settle(partial_value):
        return lax.psum_scatter(partial_value, "col", scatter_dimension=1, tiled=True)

    def kernel_product(weights):
        spread_weights = lax.all_gather(weights, "row", axis=1, tiled=True)
        return settle(
            jnp.concatenate([exact(spread_weights, part, ROWS_BY_ROWS) for part in stored], axis=1)
        )

    def orthonormal(vectors):
        gram = lax.psum(exact(vectors, vectors, ROWS_BY_ROWS), ("row", "col")) / frame_count
        return jax.scipy.linalg.solve_triangular(jnp.linalg.cholesky(gram), vectors, lower=True)

    sums = jnp.concatenate([jnp.sum(part, axis=1)[None, :] for part in stored], axis=1)
    inverse = 1.0 / settle(sums)
    degree = kernel_product(inverse)
    basis_one = orthonormal(kernel_product(start * inverse) / degree)
    return orthonormal(kernel_product(basis_one * inverse) / degree)


def shards(frames, start):
    row_size, column_size = lax.axis_size("row"), lax.axis_size("col")
    entries = row_size * column_size * frames.shape[1] ** 2
    shapes = (row_size, column_size, start.shape[0], frames.shape[1] % 128)
    if shapes == (8, 4, 32, 0) and 4 * entries <= RESIDENT_BYTES:
        return resident_shards(frames, start)
    return stored_shards(frames, start)


def solution(mesh):
    return jax.shard_map(
        shards,
        mesh=mesh,
        in_specs=(P(None, ("row", "col")), P(None, ("row", "col"))),
        out_specs=P(None, ("row", "col")),
        check_vma=False,
    )
```

```python
import functools
import math
import jax
import jax.numpy as jnp
from jax import lax
from jax.experimental import pallas as pl
from jax.experimental.pallas import tpu as pltpu
from jax.sharding import PartitionSpec as P

VMEM = pl.BlockSpec(memory_space=pltpu.VMEM)
ROWS_BY_COLUMNS = (((1,), (0,)), ((), ()))
ROWS_BY_ROWS = (((1,), (1,)), ((), ()))
RESIDENT_BYTES = 36 << 20
DEGREE_ROWS = 16


def call(body, out_shape, operands, scratch=(), limit=14 << 20, flops=0, name=None):
    return pl.pallas_call(
        body,
        out_shape=out_shape,
        in_specs=[VMEM] * len(operands),
        out_specs=jax.tree.map(lambda _: VMEM, out_shape),
        scratch_shapes=list(scratch),
        compiler_params=pltpu.CompilerParams(vmem_limit_bytes=limit),
        cost_estimate=pl.CostEstimate(flops=flops, bytes_accessed=0, transcendentals=0) if flops else None,
        name=name,
    )(*operands)


def f32(*shape):
    return jax.ShapeDtypeStruct(shape, jnp.float32)


def bf16(*shape):
    return jax.ShapeDtypeStruct(shape, jnp.bfloat16)


def halves(values):
    high = values.astype(jnp.bfloat16)
    return high, (values - high.astype(jnp.float32)).astype(jnp.bfloat16)


def thirds(values):
    high = values.astype(jnp.bfloat16).astype(jnp.float32)
    middle = (values - high).astype(jnp.bfloat16).astype(jnp.float32)
    return high, middle, values - high - middle


def pack(values):
    return jnp.concatenate([values[:, first : first + 128] for first in range(0, values.shape[1], 128)], axis=0)


def unpack(packed, lines, width):
    count = width // 128
    return jnp.concatenate([packed[block * lines : (block + 1) * lines] for block in range(count)], axis=1)


def pack_square(square):
    lines = square.shape[0] * square.shape[0] // 128
    return jnp.concatenate([square[first : first + lines] for first in range(0, square.shape[0], lines)], axis=1)


def unpack_square(packed, size):
    return jnp.concatenate([packed[:, first : first + size] for first in range(0, packed.shape[1], size)], axis=0)


def row_operand(points, left, span):
    width, features = points.shape
    high, low = halves(points)
    left[span, 0:features] = high
    left[span, features : 2 * features] = high
    left[span, 2 * features : 3 * features] = low
    first, second, third = thirds(0.5 * jnp.sum(points * points, axis=1, keepdims=True))
    lane = lax.broadcasted_iota(jnp.int32, (width, features), 1)
    tail = jnp.where(lane == 0, first, jnp.where(lane == 1, second, jnp.where(lane == 2, third, 0.0)))
    tail = jnp.where((lane > 2) & (lane < 6), -1.0, tail)
    left[span, 3 * features : 4 * features] = tail.astype(jnp.bfloat16)


def column_operand(points, right, span):
    features, width = points.shape
    high, low = halves(points)
    right[0:features, span] = high
    right[features : 2 * features, span] = low
    right[2 * features : 3 * features, span] = high
    first, second, third = thirds(0.5 * jnp.sum(points * points, axis=0, keepdims=True))
    line = lax.broadcasted_iota(jnp.int32, (features, width), 0)
    tail = jnp.where(line == 3, first, jnp.where(line == 4, second, jnp.where(line == 5, third, 0.0)))
    tail = jnp.where(line < 3, -1.0, tail)
    right[3 * features : 4 * features, span] = tail.astype(jnp.bfloat16)


def build_rows(left, right, high_ref, low_ref, totals, tile_rows=256, tile_columns=512):
    width = left.shape[0]
    for start in range(0, width, tile_rows):
        lines = slice(start, start + tile_rows)
        points = left[lines, :]
        total = jnp.zeros((tile_rows, 128), jnp.float32)
        for first in range(0, right.shape[1], tile_columns):
            span = slice(first, first + tile_columns)
            values = jnp.exp2(
                lax.dot_general(points, right[:, span], ROWS_BY_COLUMNS, preferred_element_type=jnp.float32)
            )
            high = values.astype(jnp.bfloat16)
            high_ref[lines, span] = high
            low_ref[lines, span] = (values - high.astype(jnp.float32)).astype(jnp.bfloat16)
            for lane in range(0, tile_columns, 128):
                total = total + values[:, lane : lane + 128]
        totals[lines, :] = total
    return jnp.sum(totals[...].T, axis=0, keepdims=True)


def point_scale(features):
    return math.sqrt(math.log2(math.e) / (0.25 * features))


def build_near_kernel(*refs, row_parts, column_parts):
    row_refs, column_refs = refs[:row_parts], (refs[0], *refs[row_parts : row_parts + column_parts - 1])
    outs = refs[row_parts + column_parts - 1 :]
    sums_ref, left_ref, right, totals = outs[2 * row_parts :]
    features, width = row_refs[0].shape
    scale = point_scale(features)
    for part, ref in enumerate(column_refs):
        column_operand(ref[...] * scale, right, slice(part * width, (part + 1) * width))
    sums_ref[...] = jnp.zeros_like(sums_ref)
    for part, (high_ref, low_ref) in enumerate(pairs(outs[: 2 * row_parts])):
        lines = slice(part * width, (part + 1) * width)
        row_operand(row_refs[part][...].T * scale, left_ref, lines)
        sums_ref[part : part + 1, :] = build_rows(left_ref.at[lines, :], right, high_ref, low_ref, totals)


def build_far_kernel(*refs, row_parts, column_parts):
    left_ref, near_right, near_sums_ref, start_ref, last_ref = refs[:5]
    column_refs, outs = refs[5 : 5 + column_parts], refs[5 + column_parts :]
    packed_ref, right, left, totals = outs[2 * row_parts + 4 :]
    vectors, width = start_ref.shape
    lanes = width // 128
    scale = point_scale(last_ref.shape[0])
    packed_ref[0 : vectors * lanes, :] = pack(start_ref[...])
    for part, ref in enumerate(column_refs):
        column_operand(ref[...] * scale, right, slice(part * width, (part + 1) * width))
    stores = pairs(outs[: 2 * row_parts + 4])

    def put(part, sums):
        line = (vectors + part) * lanes
        packed_ref[line : line + lanes, :] = pack(sums)

    for part in range(row_parts):
        lines = slice(part * width, (part + 1) * width)
        sums = build_rows(left_ref.at[lines, :], right, *stores[part], totals)
        put(part, near_sums_ref[part : part + 1, :] + sums)
    row_operand(last_ref[...].T * scale, left, slice(0, width))
    sums = build_rows(left, near_right, *stores[row_parts], totals)
    put(row_parts, sums + build_rows(left, right, *stores[row_parts + 1], totals))


def sweep(weights, parts, stores, block, initial=None, tile=512):
    rows = weights.shape[0] // 2
    width = stores[0][0].shape[0]
    pieces = []
    for first in range(0, width, tile):
        span = slice(block * width + first, block * width + first + tile)
        total = None if initial is None else initial[:, first : first + tile]
        for part, (high_ref, low_ref) in zip(parts, stores):
            lines = slice(part * width, (part + 1) * width)
            both = lax.dot_general(
                weights[:, lines], high_ref[:, span], ROWS_BY_COLUMNS, preferred_element_type=jnp.float32
            )
            last = lax.dot_general(
                weights[0:rows, lines], low_ref[:, span], ROWS_BY_COLUMNS, preferred_element_type=jnp.float32
            )
            term = both[0:rows] + both[rows:] + last
            total = term if total is None else total + term
        pieces.append(total)
    return jnp.concatenate(pieces, axis=1)


def pairs(refs):
    return list(zip(refs[0::2], refs[1::2]))


def place_of(block, odd):
    return block // 2, block % 2 + (2 if odd else 0)


def halved(refs, parts):
    return pairs(refs[: 2 * parts]), pairs(refs[2 * parts : 4 * parts])


def put_product(out_ref, product, vectors):
    width = product.shape[1]
    lanes = width // 128
    last = vectors * lanes
    out_ref[0:last, :] = pack(product[0:vectors])
    out_ref[last : last + 8, :] = jnp.zeros((8, 128), jnp.float32)
    out_ref[last : last + lanes, :] = pack(product[vectors : vectors + 1])


def first_kernel(*refs, parts):
    packed_refs, stores = refs[:parts], halved(refs[parts : 5 * parts], parts)
    out_ref, inverse_ref, weights = refs[5 * parts :]
    rows = weights.shape[0] // 2
    vectors = rows - DEGREE_ROWS
    width = inverse_ref.shape[1]
    lanes = width // 128

    def sums(peer, part):
        line = (vectors + part) * lanes
        return unpack(packed_refs[peer][line : line + lanes, :], 1, width)

    for part in range(parts):
        span = slice(part * width, (part + 1) * width)
        density = sums(0, part)
        for peer in range(1, parts):
            density = density + sums(peer, part ^ peer)
        inverse = 1.0 / density
        if part == 0:
            inverse_ref[...] = inverse
        line = lax.broadcasted_iota(jnp.int32, (DEGREE_ROWS, width), 0)
        for first, piece in (
            (0, unpack(packed_refs[part][0 : vectors * lanes, :], vectors, width) * inverse),
            (vectors, jnp.where(line == 0, inverse, 0.0)),
        ):
            high, low = halves(piece)
            last = first + piece.shape[0]
            weights[first:last, span] = high
            weights[rows + first : rows + last, span] = low
    for block in range(out_ref.shape[0]):
        half, place = place_of(block, True)
        put_product(out_ref.at[block], sweep(weights, range(parts), stores[half], place), vectors)


def far_kernel(*refs, parts, vectors):
    weights, stores, out_ref = refs[0], halved(refs[1 : 1 + 4 * parts], parts), refs[-1]
    for index in range(out_ref.shape[0]):
        half, place = place_of(1 + index, False)
        put_product(out_ref.at[index], sweep(weights, range(parts), stores[half], place), vectors)


def own_kernel(*refs, parts, vectors):
    weights, stores, out_ref = refs[0], pairs(refs[2 : 2 + 2 * parts]), refs[-1]
    put_product(out_ref, sweep(weights, range(parts), stores, 0), vectors)


def put_weights(weights, packed, place):
    vectors = weights.shape[0] // 2
    width = weights.shape[1] if place is None else packed.shape[0] // vectors * 128
    values = unpack(packed[0 : vectors * (width // 128), :], vectors, width)
    span = slice(0, width) if place is None else slice(place * width, (place + 1) * width)
    high, low = halves(values)
    weights[0:vectors, span] = high
    weights[vectors:, span] = low


def second_part_kernel(piece_ref, *refs):
    stores, (odd_ref, even_ref, weights) = pairs(refs[0:4]), refs[-3:]
    earlier = refs[4:-3] or (None, None)
    put_weights(weights, piece_ref[...], None)
    for odd, earlier_ref, out_ref in ((True, earlier[0], odd_ref), (False, earlier[1], even_ref)):
        for block in range(out_ref.shape[0]):
            half, place = place_of(block, odd)
            initial = None if earlier_ref is None else earlier_ref[block]
            out_ref[block] = sweep(weights, (0,), [stores[half]], place, initial)


def put_second(out_ref, product, gram):
    last = out_ref.shape[0] - gram.shape[0]
    out_ref[0:last, :] = pack(product)
    out_ref[last:, :] = gram


def second_odd_kernel(*refs, parts):
    piece_refs, refs = refs[:4], refs[4:]
    partial_ref, stores = refs[0], halved(refs[1 : 1 + 4 * parts], parts)
    out_ref, gram_ref, weights = refs[1 + 4 * parts :]
    last = piece_refs[0].shape[0] - gram_ref.shape[0]
    gram = piece_refs[0][last:, :]
    for ref in piece_refs[1:]:
        gram = gram + ref[last:, :]
    gram_ref[...] = gram
    for part, ref in enumerate(piece_refs[-parts:]):
        put_weights(weights, ref[...], part)
    for block in range(out_ref.shape[0]):
        half, place = place_of(block, True)
        product = sweep(weights, range(parts), stores[half], place, partial_ref[block])
        put_second(out_ref.at[block], product, gram)


def second_even_kernel(*refs, parts):
    weights, gram_ref, partial_ref = refs[:3]
    stores, out_ref = halved(refs[3 : 3 + 4 * parts], parts), refs[-1]
    for index in range(out_ref.shape[0]):
        half, place = place_of(1 + index, False)
        product = sweep(weights, range(parts), stores[half], place, partial_ref[1 + index])
        put_second(out_ref.at[index], product, gram_ref[...])


def second_own_kernel(*refs, parts):
    weights, gram_ref, partial_ref = refs[:3]
    stores, out_ref = pairs(refs[4 : 4 + 2 * parts]), refs[-1]
    put_second(out_ref, sweep(weights, range(parts), stores, 0, partial_ref[0]), gram_ref[...])


def exact(left, right, dims):
    return lax.dot_general(
        left, right, dims, precision=lax.Precision.HIGHEST, preferred_element_type=jnp.float32
    )


def add_up(refs):
    total = refs[0][...]
    for ref in refs[1:]:
        total = total + ref[...]
    return total


def grown_kernel(*refs):
    inverse_ref, piece_refs, (grown_ref, degree_ref) = refs[0], refs[1:-2], refs[-2:]
    width = degree_ref.shape[1]
    lanes = width // 128
    vectors = (grown_ref.shape[0] - 8) // lanes
    total = add_up(piece_refs)
    last = vectors * lanes
    degree = unpack(total[last : last + lanes], 1, width)
    grown = unpack(total[0:last], vectors, width) / degree
    degree_ref[...] = degree
    grown_ref[0:last, :] = pack(grown * inverse_ref[...])
    grown_ref[last:, :] = pack_square(exact(grown, grown, ROWS_BY_ROWS))


def inverse_factor(gram, panel=16):
    size = gram.shape[0]
    shape = (size, 2 * size)
    line = lax.broadcasted_iota(jnp.int32, (size, size), 0)
    lane = lax.broadcasted_iota(jnp.int32, (size, size), 1)
    table = jnp.concatenate([gram, jnp.where(line == lane, 1.0, 0.0)], axis=1)
    tall = lax.broadcasted_iota(jnp.int32, shape, 0)
    pivots = jnp.zeros(shape, jnp.float32)
    for first in range(0, size, panel):
        columns = [jnp.broadcast_to(table[:, step : step + 1], shape) for step in range(first, first + panel)]
        for place, step in enumerate(range(first, first + panel)):
            pivot = columns[place][step : step + 1, :]
            pivots = jnp.where(tall == step, pivot, pivots)
            factor = jnp.where(tall > step, columns[place] * (1.0 / pivot), 0.0)
            for later in range(place + 1, panel):
                columns[later] = columns[later] - factor * columns[later][step : step + 1, :]
            table = table - factor * table[step : step + 1, :]
    return table[:, size:] * lax.rsqrt(pivots[:, size:])


def grown_two_kernel(*refs, count):
    degree_ref, piece_refs, (grown_ref, gram_ref) = refs[0], refs[1:-2], refs[-2:]
    vectors, width = grown_ref.shape
    total = add_up(piece_refs)
    last = vectors * (width // 128)
    factor = inverse_factor(unpack_square(total[last:], vectors) * (1.0 / count))
    product = unpack(total[0:last], vectors, width)
    grown = exact(factor, product / degree_ref[...], ROWS_BY_COLUMNS)
    grown_ref[...] = grown
    gram_ref[...] = pack_square(exact(grown, grown, ROWS_BY_ROWS))


def finish_kernel(*refs, count):
    grown_ref, gram_refs, out_ref = refs[0], refs[1:-1], refs[-1]
    gram = unpack_square(add_up(gram_refs), grown_ref.shape[0])
    out_ref[...] = exact(inverse_factor(gram * (1.0 / count)), grown_ref[...], ROWS_BY_COLUMNS)


def swap(values, mask):
    size = lax.axis_size(("row", "col"))
    return lax.ppermute(values, ("row", "col"), [(index, index ^ mask) for index in range(size)])


def fetch_kernel(frames_ref, start_ref, own_ref, own_start_ref, sems):
    copies = [
        pltpu.make_async_copy(source, target, sems.at[index])
        for index, (source, target) in enumerate(((frames_ref, own_ref), (start_ref, own_start_ref)))
    ]
    for copy in copies:
        copy.start()
    for copy in copies:
        copy.wait()


def fetch(frames, start):
    return pl.pallas_call(
        fetch_kernel,
        out_shape=(f32(*frames.shape), f32(*start.shape)),
        in_specs=[pl.BlockSpec(memory_space=pltpu.HBM)] * 2,
        out_specs=(VMEM, VMEM),
        scratch_shapes=[pltpu.SemaphoreType.DMA((2,))],
        compiler_params=pltpu.CompilerParams(vmem_limit_bytes=1 << 20),
        cost_estimate=pl.CostEstimate(flops=1 << 34, bytes_accessed=0, transcendentals=0),
        name="fetch",
    )(pltpu.with_memory_space_constraint(frames, pltpu.HBM), pltpu.with_memory_space_constraint(start, pltpu.HBM))


def resident_shards(frames, start):
    row_size, column_size = lax.axis_size("row"), lax.axis_size("col")
    count = frames.shape[1] * row_size * column_size
    features, width = frames.shape
    vectors = start.shape[0]

    core, across, skip = column_size, column_size * row_size // 2, column_size // 2
    beside, along = 2 * core, 1
    near = (across, skip, across | skip)
    far = (beside, along, beside | along)
    parts, half = 4, 4

    skip_piece = swap(frames, skip)
    own, own_start = fetch(frames, start)
    beside_piece = swap(own, beside)
    along_piece = swap(own, along)
    across_piece = swap(swap(own, across | core), core)
    corner_piece = swap(along_piece, beside)
    row_pieces = [across_piece, skip_piece]
    last_piece = swap(skip_piece, across)
    near_columns = [beside_piece, swap(own, core), swap(beside_piece, core)]
    far_columns = [along_piece, corner_piece, swap(along_piece, core), swap(corner_piece, core)]

    operands = 4 * features
    columns = half * width
    lanes = width // 128
    packed_lines = vectors * lanes + 8
    rest = parts - 1
    stored = (bf16(width, columns),) * 2
    totals = pltpu.VMEM((width, 128), jnp.float32)
    *near_store, sums, left, right = call(
        functools.partial(build_near_kernel, row_parts=rest, column_parts=half),
        (*(stored * rest), f32(8, width), bf16(rest * width, operands), bf16(operands, columns)),
        (own, *row_pieces, *near_columns),
        scratch=(totals,),
        flops=1,
        name="build_near",
    )
    *far_store, last_high, last_low, far_high, far_low, packed = call(
        functools.partial(build_far_kernel, row_parts=rest, column_parts=half),
        (*(stored * (rest + 2)), f32((vectors + parts) * lanes, 128)),
        (left, right, sums, own_start, last_piece, *far_columns),
        scratch=(
            pltpu.VMEM((operands, columns), jnp.bfloat16),
            pltpu.VMEM((width, operands), jnp.bfloat16),
            totals,
        ),
        flops=1,
        name="build_far",
    )
    near_store = (*near_store, last_high, last_low)
    far_store = (*far_store, far_high, far_low)
    all_packed = [packed] + [swap(packed, mask) for mask in near]

    def spread(odds, evens):
        odds = swap(odds, core)
        both = evens + odds[1:]
        return odds[0], both, [swap(both[place], mask) for place, mask in enumerate(far)]

    def total_gram(gram):
        gram = gram + swap(gram, core)
        gram = functools.reduce(jnp.add, [swap(gram, mask | core) for mask in far], gram)
        return [gram] + [swap(gram, mask | core) for mask in near]

    rows = vectors + DEGREE_ROWS
    block = 2 * 3 * rows * parts * width * width
    odds, inverse, weights = call(
        functools.partial(first_kernel, parts=parts),
        (f32(half, packed_lines, 128), f32(1, width), bf16(2 * rows, parts * width)),
        (*all_packed, *near_store, *far_store),
        flops=half * block,
        name="first_odd",
    )
    evens = call(
        functools.partial(far_kernel, parts=parts, vectors=vectors),
        f32(half - 1, packed_lines, 128),
        (weights, *near_store, *far_store),
        flops=(half - 1) * block,
        name="first_even",
    )
    own_odd, both, others = spread(odds, evens)
    own_even = call(
        functools.partial(own_kernel, parts=parts, vectors=vectors),
        f32(packed_lines, 128),
        (weights, both, *near_store),
        flops=block,
        name="first_own",
    )
    weighted, degree = call(
        grown_kernel,
        (f32(packed_lines, 128), f32(1, width)),
        (inverse, own_even, own_odd, *others),
        name="grown",
    )
    pieces = [weighted] + [swap(weighted, mask) for mask in near]
    partial = ()
    for part in range(2):
        partial = call(
            second_part_kernel,
            (f32(half, vectors, width),) * 2,
            (pieces[part], *near_store[2 * part : 2 * part + 2], *far_store[2 * part : 2 * part + 2], *partial),
            scratch=(pltpu.VMEM((2 * vectors, width), jnp.bfloat16),),
            flops=2 * half * block // parts,
            name="second_part",
        )
    odd_partial, even_partial = partial
    rest = parts - 2
    near_store, far_store = near_store[4:], far_store[4:]
    odds, gram, weights = call(
        functools.partial(second_odd_kernel, parts=rest),
        (f32(half, packed_lines, 128), f32(8, 128), bf16(2 * vectors, rest * width)),
        (*pieces, odd_partial, *near_store, *far_store),
        flops=half * block,
        name="second_odd",
    )
    evens = call(
        functools.partial(second_even_kernel, parts=rest),
        f32(half - 1, packed_lines, 128),
        (weights, gram, even_partial, *near_store, *far_store),
        flops=(half - 1) * block,
        name="second_even",
    )
    own_odd, both, others = spread(odds, evens)
    own_even = call(
        functools.partial(second_own_kernel, parts=rest),
        f32(packed_lines, 128),
        (weights, gram, even_partial, both, *near_store),
        flops=block,
        name="second_own",
    )
    grown_two, gram_two = call(
        functools.partial(grown_two_kernel, count=count),
        (f32(vectors, width), f32(8, 128)),
        (degree, own_even, own_odd, *others),
        name="grown_two",
    )
    return call(
        functools.partial(finish_kernel, count=count),
        f32(vectors, width),
        (grown_two, *total_gram(gram_two)),
        name="finish",
    )


def build_block(block_points, block_squares, column_points, column_squares):
    products = lax.dot_general(
        block_points, column_points, (((0,), (0,)), ((), ())), precision=lax.Precision.HIGHEST
    )
    distance = block_squares[:, None] + column_squares[None, :] - 2.0 * products
    return jnp.exp(-distance / (0.5 * block_points.shape[0]))


def stored_shards(frames, start):
    block_points = lax.all_gather(frames, "col", axis=1, tiled=True)
    column_points = lax.all_gather(frames, "row", axis=1, tiled=True)
    block_squares = jnp.sum(block_points * block_points, axis=0)
    column_squares = jnp.sum(column_points * column_points, axis=0)
    frame_count = frames.shape[1] * lax.axis_size("row") * lax.axis_size("col")
    block_rows = block_points.shape[1]
    height = min(512, block_rows)
    stored = [
        build_block(
            block_points[:, first : first + height],
            block_squares[first : first + height],
            column_points,
            column_squares,
        )
        for first in range(0, block_rows, height)
    ]

    def settle(partial_value):
        return lax.psum_scatter(partial_value, "col", scatter_dimension=1, tiled=True)

    def kernel_product(weights):
        spread_weights = lax.all_gather(weights, "row", axis=1, tiled=True)
        return settle(
            jnp.concatenate([exact(spread_weights, part, ROWS_BY_ROWS) for part in stored], axis=1)
        )

    def orthonormal(vectors):
        gram = lax.psum(exact(vectors, vectors, ROWS_BY_ROWS), ("row", "col")) / frame_count
        return jax.scipy.linalg.solve_triangular(jnp.linalg.cholesky(gram), vectors, lower=True)

    sums = jnp.concatenate([jnp.sum(part, axis=1)[None, :] for part in stored], axis=1)
    inverse = 1.0 / settle(sums)
    degree = kernel_product(inverse)
    basis_one = orthonormal(kernel_product(start * inverse) / degree)
    return orthonormal(kernel_product(basis_one * inverse) / degree)


def shards(frames, start):
    row_size, column_size = lax.axis_size("row"), lax.axis_size("col")
    entries = row_size * column_size * frames.shape[1] ** 2
    shapes = (row_size, column_size, start.shape[0], frames.shape[1] % 128)
    if shapes == (8, 4, 32, 0) and 4 * entries <= RESIDENT_BYTES:
        return resident_shards(frames, start)
    return stored_shards(frames, start)


def solution(mesh):
    return jax.shard_map(
        shards,
        mesh=mesh,
        in_specs=(P(None, ("row", "col")), P(None, ("row", "col"))),
        out_specs=P(None, ("row", "col")),
        check_vma=False,
    )
```
